32 devices in a mesh: dp: 4 (over y, x), proto: 8 (over z, core).
Axes of the slice: x: 2, y: 2, z: 4, core: 2. Of those that a mesh axis runs over, the one named last changes fastest.
Arguments:
- student_patch: bfloat16 [4, 1024, 256], P('dp', 'proto'), may hold values from -4 to 4
- teacher_patch: bfloat16 [4, 1024, 256], P('dp', 'proto'), may hold values from -4 to 4
- patch_image: int32 [4, 1024], P('dp', 'proto'), may hold values from 0 to 3, never falling along the last dimension, each value on 1 to 512 neighbouring positions
- masked_rows: int32 [4, 512], P('dp', 'proto'), may hold values from 0 to 127, as said below
- student_proto: float32 [256, 131072], P(None, 'proto'), as said below
- teacher_proto: float32 [256, 131072], P(None, 'proto'), as said below
- first_moment: float32 [256, 131072], P('dp', 'proto'), as said below
- second_moment: float32 [256, 131072], P('dp', 'proto'), as said below
- centre: float32 [131072], P('proto'), may hold values from -0.3 to 0.3
Outputs:
- row_grad: float32 [4, 512, 256], P('dp', 'proto')
- new_student: float32 [256, 131072], P('dp', 'proto')
- new_first: float32 [256, 131072], P('dp', 'proto')
- new_second: float32 [256, 131072], P('dp', 'proto')
- new_teacher: float32 [256, 131072], P('dp', 'proto')
- loss: float32 [], replicated
The draws below stay inside these ranges and needn't reach their ends.
Inputs may be any that keep to these rules, and one draw needn't show every extreme that they name: `masked_rows`: for each data group and each index of proto in order, 64 distinct positions among that device's 128 patches, ascending; position 0 and position 127 of every device are always masked. `student_proto`: finite entries. `teacher_proto`: finite entries. `first_moment`: finite entries. `second_moment`: positive entries.
All inputs are finite; a program needn't handle non-finite values.
Results may differ from the reference program's by a relative error of at most 0.014.
Values may be sent and summed in bfloat16 or wider, within the bound.
No kernel may reach another device: no remote copies, remote signals or barrier semaphores. Data moves between devices by JAX's collectives and lax.ppermute only.
A program may use at most 256 MiB of HBM per device.

```python
import math
import jax
import jax.numpy as jnp
import numpy as np
from jax import lax

E = 256
K = 131072
MASK_DEV = 64
PATCH_IMG = 256
PATCH_DEV = 128
ROWS_GROUP = 512
ROWS = 2048
IMG_GROUP = 4
IMAGES = 16
K_DEV = 16384
N_DP = 4
N_PROTO = 8


def group_mix():
    place = jnp.arange(N_DP, dtype=jnp.float32) / max(N_DP - 1, 1)
    return 0.95 * place


def common_noise(key):
    return jax.random.normal(jax.random.fold_in(key, 11), (N_DP, PATCH_DEV * N_PROTO, E), jnp.float32)


def student_rows(key):
    values = common_noise(key)
    return jnp.clip(values, -4.0, 4.0)


def teacher_rows(key):
    subkey = jax.random.fold_in(key, 12)
    own = jnp.clip(jax.random.normal(subkey, (N_DP, PATCH_DEV * N_PROTO, E), jnp.float32), -1.5, 1.5)
    mix = group_mix()[:, None, None]
    values = mix * common_noise(key) + jnp.sqrt(1.0 - mix * mix) * own
    return jnp.clip(values, -4.0, 4.0)


def column_scale(key):
    phase = jax.random.uniform(jax.random.fold_in(key, 23), (), jnp.float32, 0.0, 2.0 * math.pi)
    place = jnp.arange(K, dtype=jnp.float32) / K
    return jnp.exp(0.25 * jnp.sin(2.0 * math.pi * place + phase))


def base_table(key):
    table = jnp.clip(jax.random.normal(jax.random.fold_in(key, 21), (E, K), jnp.float32), -4.0, 4.0)
    return table * 0.0625 * column_scale(key)[None, :]


def add_spikes(table):
    return table


def grad_scale():
    return 20.0 * math.sqrt(ROWS) / (K * math.sqrt(E))


def draw_student_patch(key, part):
    return student_rows(key).astype(jnp.bfloat16)


def draw_teacher_patch(key, part):
    return teacher_rows(key).astype(jnp.bfloat16)


def draw_student_proto(key, part):
    return add_spikes(base_table(key))


def draw_teacher_proto(key, part):
    drift = jnp.clip(jax.random.normal(jax.random.fold_in(key, 22), (E, K), jnp.float32), -3.0, 3.0) * 0.0125
    return add_spikes(base_table(key) + drift)


def draw_centre(key, part):
    phase = jax.random.uniform(jax.random.fold_in(key, 51), (), jnp.float32, 0.0, 2.0 * math.pi)
    place = jnp.arange(K, dtype=jnp.float32) / K
    subkey = jax.random.fold_in(key, 52)
    amplitude = 0.5
    rough = jnp.clip(jax.random.normal(subkey, (K,), jnp.float32), -3.0, 3.0) * 0.02
    values = 0.07 * amplitude * jnp.sin(2.0 * math.pi * place + phase) + rough
    return values


def draw_masked_rows(key, part):
    device_keys = jax.random.split(jax.random.fold_in(key, 31), N_DP * N_PROTO)

    def one_device(device_key):
        middle = jax.random.permutation(device_key, PATCH_DEV - 2).astype(jnp.int32) + 1
        chosen = jnp.concatenate([jnp.zeros((1,), jnp.int32), middle[:MASK_DEV - 2], jnp.full((1,), PATCH_DEV - 1, jnp.int32)])
        return jnp.sort(chosen).astype(jnp.int32)
    picked = jax.vmap(one_device)(device_keys)
    return picked.reshape(N_DP, N_PROTO * MASK_DEV).astype(jnp.int32)


def draw_first_moment(key, part):
    subkey = jax.random.fold_in(key, 41)
    values = jnp.clip(jax.random.normal(subkey, (E, K), jnp.float32), -5.0, 5.0) * 0.25
    return values * grad_scale()


def draw_second_moment(key, part):
    subkey = jax.random.fold_in(key, 42)
    spread = jax.random.uniform(subkey, (E, K), jnp.float32, math.log(0.25), math.log(4.0))
    return jnp.exp(spread) * (0.095 * grad_scale() * grad_scale())


def profile(number_of, total, reach, lean):
    portions = [(1 << 20) // math.isqrt(grade ** lean) + 1 for grade in range(2, number_of + 1)]
    spare, given = total - reach - (number_of - 1), [1] * (number_of - 1)
    while spare > 0:
        candidates = [i for i in range(number_of - 1) if given[i] < reach]
        mass, left = sum([portions[i] for i in candidates]), spare
        for i in candidates:
            extra = min(reach - given[i], max(1, left * portions[i] // mass), spare)
            given[i] = given[i] + extra
            spare = spare - extra
    return np.array([reach] + given)


def ragged_sizes(own_key, amount, total, most, slope):
    if amount == 2:
        one = jax.random.randint(own_key, (), max(1, total - most), min(most, total - 1) + 1)
        return jnp.stack([one, total - one])
    tallies = jnp.asarray(profile(amount, total, most, slope), jnp.int32)
    couples = (amount - 1) // 2
    source_of, receiver = tallies[1:1 + 2 * couples:2], tallies[2:2 + 2 * couples:2]
    slack = jnp.minimum(source_of - 1, most - receiver)
    passed = jax.random.randint(jax.random.fold_in(own_key, 1), (couples,), 0, 1 << 20) % (slack + 1)
    tallies = tallies.at[1:1 + 2 * couples:2].set(source_of - passed).at[2:2 + 2 * couples:2].set(receiver + passed)
    return tallies[jax.random.permutation(jax.random.fold_in(own_key, 2), amount)]


def setup_inputs(seed: int = 0) -> dict:
    key_of = jax.random.split(jax.random.key(seed), 10)
    return {
        "student_patch": draw_student_patch(jax.random.fold_in(key_of[9], 71), 0),
        "teacher_patch": draw_teacher_patch(jax.random.fold_in(key_of[9], 71), 0),
        "patch_image": jax.vmap(lambda own: jnp.searchsorted(jnp.cumsum(ragged_sizes(own, IMG_GROUP, PATCH_DEV * N_PROTO, 2 * PATCH_IMG, 1)), jnp.arange(PATCH_DEV * N_PROTO), side="right"))(jax.random.split(key_of[2], N_DP)).reshape((N_DP, PATCH_DEV * N_PROTO)).astype(jnp.int32),
        "masked_rows": draw_masked_rows(jax.random.fold_in(key_of[9], 71), 0),
        "student_proto": draw_student_proto(jax.random.fold_in(key_of[9], 71), 0),
        "teacher_proto": draw_teacher_proto(jax.random.fold_in(key_of[9], 71), 0),
        "first_moment": draw_first_moment(jax.random.fold_in(key_of[9], 71), 0),
        "second_moment": draw_second_moment(jax.random.fold_in(key_of[9], 71), 0),
        "centre": draw_centre(jax.random.fold_in(key_of[9], 71), 0),
    }


student_temp = 0.1
teacher_temp = 0.07
beta_one = 0.9
beta_two = 0.999
fix_one = 0.9999734386011124
fix_two = 0.09520785288629038
learn_rate = 0.002
decay_rate = 0.04
teacher_keep = 0.994

def unit_rows(raw_rows):
    inverse = lax.rsqrt(lax.optimization_barrier(jnp.sum(raw_rows * raw_rows, axis=-1, keepdims=True)) + 1e-06)
    return (raw_rows * inverse, inverse)

def reference(student_patch, teacher_patch, patch_image, masked_rows, student_proto, teacher_proto, first_moment, second_moment, centre):
    offsets = (jnp.arange(ROWS_GROUP, dtype=jnp.int32) // MASK_DEV * PATCH_DEV).astype(jnp.int32)
    places = (masked_rows + offsets[None, :]).astype(jnp.int32)
    pick_rows = jax.vmap(lambda patch_table, row_where: patch_table[row_where])
    raw_student = pick_rows(student_patch, places).astype(jnp.float32)
    raw_teacher = pick_rows(teacher_patch, places).astype(jnp.float32)
    image_ids = pick_rows(patch_image, places)
    unit_student, inv_student = unit_rows(raw_student)
    unit_teacher, inv_teacher = unit_rows(raw_teacher)
    rows_student = unit_student.astype(jnp.bfloat16).reshape(ROWS, E)
    rows_teacher = unit_teacher.astype(jnp.bfloat16).reshape(ROWS, E)
    labels = jnp.arange(IMG_GROUP, dtype=jnp.int32)
    matches = (image_ids[:, :, None] == labels[None, None, :]).astype(jnp.float32)
    counts = lax.optimization_barrier(jnp.sum(matches, axis=1))
    per_row = jnp.einsum('gri,gi->gr', matches, counts, precision=lax.Precision.HIGHEST)
    weights = (ROWS / IMAGES / per_row).reshape(ROWS)
    student_w = student_proto.astype(jnp.bfloat16)
    teacher_w = teacher_proto.astype(jnp.bfloat16)

    def logits(block_index):
        first_col = block_index * K_DEV
        ws_block = lax.dynamic_slice_in_dim(student_w, first_col, K_DEV, 1)
        wt_block = lax.dynamic_slice_in_dim(teacher_w, first_col, K_DEV, 1)
        centre_block = lax.dynamic_slice_in_dim(centre, first_col, K_DEV, 0)
        student_logit = jnp.dot(rows_student, ws_block, preferred_element_type=jnp.float32) / student_temp
        teacher_raw = jnp.dot(rows_teacher, wt_block, preferred_element_type=jnp.float32)
        teacher_logit = (teacher_raw - centre_block) / teacher_temp
        return (student_logit, teacher_logit, ws_block)

    def first_pass(state_in, block_index):
        peak_s, sum_s, peak_t, sum_t = state_in
        student_logit, teacher_logit, ws_block = logits(block_index)
        new_peak_s = jnp.maximum(peak_s, lax.optimization_barrier(jnp.max(student_logit, axis=1)))
        new_peak_t = jnp.maximum(peak_t, lax.optimization_barrier(jnp.max(teacher_logit, axis=1)))
        sum_s = sum_s * jnp.exp(peak_s - new_peak_s) + lax.optimization_barrier(jnp.sum(jnp.exp(student_logit - new_peak_s[:, None]), axis=1))
        sum_t = sum_t * jnp.exp(peak_t - new_peak_t) + lax.optimization_barrier(jnp.sum(jnp.exp(teacher_logit - new_peak_t[:, None]), axis=1))
        return ((new_peak_s, sum_s, new_peak_t, sum_t), None)
    lowest = jnp.full((ROWS,), -jnp.inf, jnp.float32)
    nothing = jnp.zeros((ROWS,), jnp.float32)
    block_ids = jnp.arange(N_PROTO, dtype=jnp.int32)
    (peak_s, sum_s, peak_t, sum_t), unused = lax.scan(first_pass, (lowest, nothing, lowest, nothing), block_ids)
    log_total = peak_s + jnp.log(sum_s)

    def second_pass(state_in, block_index):
        loss_acc, unit_grad = state_in
        student_logit, teacher_logit, ws_block = logits(block_index)
        prob_s = jnp.exp(student_logit - peak_s[:, None]) / sum_s[:, None]
        prob_t = jnp.exp(teacher_logit - peak_t[:, None]) / sum_t[:, None]
        loss_acc = loss_acc + jnp.sum(weights * lax.optimization_barrier(jnp.sum(prob_t * (log_total[:, None] - student_logit), axis=1)))
        grad_logit = (weights[:, None] * (prob_s - prob_t) / student_temp).astype(jnp.bfloat16)
        unit_grad = unit_grad + lax.dot_general(grad_logit, ws_block, (((1,), (1,)), ((), ())), preferred_element_type=jnp.float32)
        partial_value = jnp.einsum('gre,grk->gek', rows_student.reshape(N_DP, ROWS_GROUP, E).astype(jnp.float32), grad_logit.reshape(N_DP, ROWS_GROUP, K_DEV).astype(jnp.float32))
        rounded = lax.optimization_barrier(partial_value.astype(jnp.bfloat16))
        return ((loss_acc, unit_grad), lax.optimization_barrier(jnp.sum(rounded.astype(jnp.float32), axis=0)))
    start_state = (jnp.zeros((), jnp.float32), jnp.zeros((ROWS, E), jnp.float32))
    (loss_acc, unit_grad), grad_parts = lax.scan(second_pass, start_state, block_ids)
    proto_grad = jnp.transpose(grad_parts, (1, 0, 2)).reshape(E, K)
    unit_grad = unit_grad.reshape(N_DP, ROWS_GROUP, E)
    row_grad = inv_student * unit_grad - inv_student * inv_student * inv_student * raw_student * lax.optimization_barrier(jnp.sum(raw_student * unit_grad, axis=-1, keepdims=True))
    new_first = beta_one * first_moment + (1.0 - beta_one) * proto_grad
    new_second = beta_two * second_moment + (1.0 - beta_two) * proto_grad * proto_grad
    step_size = new_first / fix_one / (jnp.sqrt(new_second / fix_two) + 1e-08)
    new_student = student_proto - learn_rate * (step_size + decay_rate * student_proto)
    new_teacher = teacher_keep * teacher_proto + (1.0 - teacher_keep) * new_student
    loss = loss_acc / ROWS
    return (row_grad, new_student, new_first, new_second, new_teacher, loss)
```

```python
import functools

import jax
import jax.numpy as jnp
from jax import lax
from jax.experimental import pallas as pl
from jax.experimental.pallas import tpu as pltpu
from jax.sharding import PartitionSpec as P

PATCH_IMG = 256

student_temp = 0.1
teacher_temp = 0.07
beta_one = 0.9
beta_two = 0.999
fix_one = 0.9999734386011124
fix_two = 0.09520785288629038
learn_rate = 0.002
decay_rate = 0.04
teacher_keep = 0.994

log2_e = 1.4426950408889634
ln_2 = 0.6931471805599453
scale_s = log2_e / student_temp
scale_t = log2_e / teacher_temp

f32 = jnp.float32
bf16 = jnp.bfloat16
PAD = 16
VMEM_LIMIT = 56 << 20
CHUNKS = 2


def params(**more):
    return pltpu.CompilerParams(vmem_limit_bytes=VMEM_LIMIT, **more)


def whole(shape):
    return pl.BlockSpec(shape, lambda *_: (0,) * len(shape))


def xor_pairs(size, k):
    return [(i, i ^ k) for i in range(size)]


def pick_kernel(rows_ref, image_ref, student_ref, teacher_ref, pack_ref, raw_ref, inv_ref):
    patches, width = student_ref.shape
    count = rows_ref.shape[1]
    hot = lax.broadcasted_iota(jnp.int32, (patches, count), 0) == rows_ref[...]
    hot = jnp.where(hot, 1.0, 0.0).astype(bf16)

    def pick(table):
        return lax.dot_general(hot, table, (((0,), (0,)), ((), ())), preferred_element_type=f32)

    def unit(raw):
        inverse = lax.rsqrt(jnp.sum(raw * raw, axis=-1, keepdims=True) + 1e-06)
        return raw * inverse, inverse

    raw_s = pick(student_ref[...])
    unit_s, inv_s = unit(raw_s)
    unit_t, _ = unit(pick(teacher_ref[...]))
    raw_ref[...] = raw_s
    inv_ref[...] = jnp.broadcast_to(inv_s, inv_ref.shape)
    pack_ref[0:count, :] = unit_s.astype(bf16)
    pack_ref[count : 2 * count, :] = unit_t.astype(bf16)
    images = jnp.broadcast_to(image_ref[...].astype(f32), (PAD, patches)).astype(bf16)
    ids = jnp.dot(images, hot, preferred_element_type=f32)
    pack_ref[2 * count :, :] = jnp.zeros((PAD, width), bf16)
    pack_ref[2 * count :, 0:count] = ids.astype(bf16)


def pick_rows(rows, image, student, teacher):
    patches, width = student.shape
    count = rows.shape[1]
    return pl.pallas_call(
        pick_kernel,
        out_shape=[
            jax.ShapeDtypeStruct((2 * count + PAD, width), bf16),
            jax.ShapeDtypeStruct((count, width), f32),
            jax.ShapeDtypeStruct((count, 128), f32),
        ],
        compiler_params=params(),
        name="pick_rows",
    )(rows, image, student, teacher)


def first_kernel(own_ref, other_ref, ws_ref, wt_ref, centre_ref, out_ref, us, ut, ms, ss, mt, st, *, count):
    step = pl.program_id(0)
    pack = 2 * count + PAD
    rows = us.shape[0]
    half = rows // 2
    cols = ws_ref.shape[1]

    @pl.when(step == 0)
    def _():
        for c, ref in enumerate((own_ref, other_ref)):
            for z in range(half // count):
                at = c * half + z * count
                us[at : at + count, :] = ref[z * pack : z * pack + count, :]
                ut[at : at + count, :] = ref[z * pack + count : z * pack + 2 * count, :]
        for m, s in ((ms, ss), (mt, st)):
            m[...] = jnp.full_like(m, -jnp.inf)
            s[...] = jnp.zeros_like(s)

    def update(parts, m_ref, s_ref, at):
        old = m_ref[at, :]
        new = functools.reduce(jnp.maximum, parts, old)
        total = functools.reduce(jnp.add, [jnp.exp2(part - new) for part in parts])
        s_ref[at, :] = s_ref[at, :] * jnp.exp2(old - new) + total
        m_ref[at, :] = new

    block = min(rows, 512)
    tile = min(cols, 1024)
    for t in range(cols // tile):
        span = slice(t * tile, (t + 1) * tile)
        ws = ws_ref[:, span].astype(bf16)
        wt = wt_ref[:, span].astype(bf16)
        shift = centre_ref[:, span] * scale_t
        for r in range(rows // block):
            at = slice(r * block, (r + 1) * block)
            zs = jnp.dot(us[at, :], ws, preferred_element_type=f32)
            update([zs[:, i : i + 128] * scale_s for i in range(0, tile, 128)], ms, ss, at)
            zt = jnp.dot(ut[at, :], wt, preferred_element_type=f32)
            update([zt[:, i : i + 128] * scale_t - shift[:, i : i + 128] for i in range(0, tile, 128)], mt, st, at)

    @pl.when(step == pl.num_programs(0) - 1)
    def _():
        out_ref[...] = jnp.zeros_like(out_ref)
        for k, (m, s) in enumerate(((ms, ss), (mt, st))):
            lanes = m[...]
            peak = jnp.max(lanes, axis=1, keepdims=True)
            total = jnp.sum(s[...] * jnp.exp2(lanes - peak), axis=1, keepdims=True)
            lse = jnp.broadcast_to(peak + jnp.log2(total), lanes.shape)
            out_ref[k : k + 1, :] = jnp.transpose(lse)[0:1, :]


def first_pass(own, other, ws, wt, centre, count):
    width, cols = ws.shape
    rows = 2 * own.shape[0] // (2 * count + PAD) * count
    tile = min(cols, 2048)
    return pl.pallas_call(
        functools.partial(first_kernel, count=count),
        grid=(cols // tile,),
        in_specs=[
            whole(own.shape),
            whole(other.shape),
            pl.BlockSpec((width, tile), lambda j: (0, j)),
            pl.BlockSpec((width, tile), lambda j: (0, j)),
            pl.BlockSpec((1, tile), lambda j: (0, j)),
        ],
        out_specs=whole((8, rows)),
        out_shape=jax.ShapeDtypeStruct((8, rows), f32),
        scratch_shapes=[pltpu.VMEM((rows, width), bf16)] * 2 + [pltpu.VMEM((rows, 128), f32)] * 4,
        compiler_params=params(),
        cost_estimate=pl.CostEstimate(flops=4 * rows * width * cols, bytes_accessed=8 * width * cols, transcendentals=2 * rows * cols),
        name="first_pass",
    )(own, other, ws, wt, centre)


def join(parts):
    peak = functools.reduce(jnp.maximum, parts)
    total = functools.reduce(jnp.add, [jnp.exp2(part - peak) for part in parts])
    return peak + jnp.log2(total)


def swap_blocks(x, k, size):
    n = x.shape[1] // size
    return jnp.concatenate([x[:, (j ^ k) * size : ((j ^ k) + 1) * size] for j in range(n)], axis=1)


def core_join_kernel(own_ref, other_ref, out_ref):
    half = own_ref.shape[1] // 2
    out_ref[...] = join([own_ref[...], swap_blocks(other_ref[...], 1, half)])


def final_join_kernel(*refs, count, images, ratio):
    stats, (own_ref, other_ref), (out_ref, loss_ref) = refs[:-4], refs[-4:-2], refs[-2:]
    rows = stats[0].shape[1]
    pack = 2 * count + PAD
    lse = join([swap_blocks(ref[...], k, count) for k, ref in enumerate(stats)])
    ids = jnp.concatenate(
        [
            ref[z * pack + 2 * count : (z + 1) * pack, 0:count].astype(f32)[0:8, :]
            for ref in (own_ref, other_ref)
            for z in range(rows // (2 * count))
        ],
        axis=1,
    )
    per_row = jnp.zeros_like(ids)
    for label in range(images):
        match = jnp.where(ids == label, 1.0, 0.0)
        per_row += match * jnp.sum(match, axis=1, keepdims=True)
    weight = ratio / per_row
    out_ref[...] = lse - jnp.log2(weight / student_temp)
    own = jnp.sum(weight[0:1, 0:count] * lse[0:1, 0:count] * ln_2, axis=1, keepdims=True)
    loss_ref[...] = jnp.broadcast_to(own, loss_ref.shape)


def lay_kernel(slab_ref, *refs, count, groups):
    packs, us, ut, flipped, turned = refs[: 2 * groups], refs[-4], refs[-3], refs[-2], refs[-1]
    pack = 2 * count + PAD
    zs = packs[0].shape[0] // pack
    at = 0
    for g in range(groups):
        for c in range(2):
            ref = packs[2 * g + c]
            for z in range(zs):
                us[at : at + count, :] = ref[z * pack : z * pack + count, :]
                ut[at : at + count, :] = ref[z * pack + count : z * pack + 2 * count, :]
                at += count
    width = us.shape[1]
    turned[...] = jnp.transpose(us[...])
    slab = width // groups
    for k in range(groups):
        start = pl.multiple_of((slab_ref[0] ^ k) * slab, slab)
        flipped[k * slab : (k + 1) * slab, :] = turned[pl.ds(start, slab), :]


def lay_rows(slab, packs, count):
    groups = len(packs) // 2
    width = packs[0].shape[1]
    rows = 2 * groups * (packs[0].shape[0] // (2 * count + PAD)) * count
    return pl.pallas_call(
        functools.partial(lay_kernel, count=count, groups=groups),
        in_specs=[pl.BlockSpec(memory_space=pltpu.SMEM)] + [pl.BlockSpec(memory_space=pltpu.VMEM)] * len(packs),
        out_shape=[jax.ShapeDtypeStruct((rows, width), bf16)] * 2 + [jax.ShapeDtypeStruct((width, rows), bf16)],
        scratch_shapes=[pltpu.VMEM((width, rows), bf16)],
        compiler_params=params(),
        name="lay_rows",
    )(slab, *packs)


def second_kernel(place_ref, us, ut, flipped, ws_ref, wt_ref, centre_ref, *refs, groups, first, last, count):
    stats = refs[:groups]
    refs = refs[groups:]
    if first:
        carry_ref = seed_ref = None
    else:
        carry_ref, seed_ref = refs[:2]
        refs = refs[2:]
    grads, refs = refs[:groups], refs[groups:]
    if last:
        keep_ref, send_ref, loss_ref, total, loss_sum, shift_s, shift_t = refs
    else:
        total, loss_ref, loss_sum, shift_s, shift_t = refs
    step = pl.program_id(0)
    rows, width = us.shape
    group_rows = rows // groups
    tile = ws_ref.shape[1]

    @pl.when(step == 0)
    def _():
        total[...] = jnp.zeros_like(total) if first else carry_ref[...]
        loss_sum[...] = jnp.zeros_like(loss_sum)
        for g in range(groups):
            at = slice(g * group_rows, (g + 1) * group_rows)
            for k, shift in enumerate((shift_s, shift_t)):
                line = jnp.broadcast_to(stats[g][k : k + 1, :], (128, group_rows))
                shift[at, :] = jnp.transpose(line)

    ws = ws_ref[...].astype(bf16)
    wt = wt_ref[...].astype(bf16)
    centre = centre_ref[...] * scale_t
    block = min(group_rows, 512)
    grad = None
    for r in range(rows // block):
        at = slice(r * block, (r + 1) * block)
        zs = jnp.dot(us[at, :], ws, preferred_element_type=f32)
        zt = jnp.dot(ut[at, :], wt, preferred_element_type=f32)
        as_, at_ = shift_s[at, :], shift_t[at, :]
        parts = []
        loss = None
        for i in range(0, tile, 128):
            zsi = zs[:, i : i + 128]
            ps = jnp.exp2(zsi * scale_s - as_)
            pt = jnp.exp2(zt[:, i : i + 128] * scale_t - centre[:, i : i + 128] - at_)
            cross = pt * zsi
            loss = cross if loss is None else loss + cross
            parts.append((ps - pt).astype(bf16))
        loss_sum[...] += jnp.sum(loss.reshape(block // 8, 8, 128), axis=0)
        logit = jnp.concatenate(parts, axis=1)
        total[at, :] += lax.dot_general(logit, ws, (((1,), (1,)), ((), ())), preferred_element_type=f32)
        part = jnp.dot(flipped[:, at], logit, preferred_element_type=f32)
        grad = part if grad is None else grad + part
    slab = width // groups
    for k in range(groups):
        grads[k][...] = grad[k * slab : (k + 1) * slab, :].astype(bf16)

    @pl.when(step == pl.num_programs(0) - 1)
    def _():
        done = jnp.sum(jnp.sum(loss_sum[...], axis=1, keepdims=True), axis=0, keepdims=True)
        loss = jnp.broadcast_to(done, loss_ref.shape)
        if not first:
            loss += seed_ref[...]
        loss_ref[...] = loss
        if last:
            zs_count = group_rows // (2 * count)
            for g in range(groups):
                for c, ref in enumerate((keep_ref, send_ref)):
                    for z in range(zs_count):
                        src = g * group_rows + (c * zs_count + z) * count
                        dst = (z * groups + g) * count
                        ref[dst : dst + count, :] = total[src : src + count, :].astype(ref.dtype)


def second_pass(place, us, ut, flipped, ws, wt, centre, stats, carry, index, chunks, share, count):
    rows, width = us.shape
    groups = len(stats)
    slab = width // groups
    chunk = share // chunks
    tile = min(chunk, 512)
    steps = chunk // tile
    first, last = index == 0, index == chunks - 1
    column = lambda j, place_ref: (0, place_ref[0] * (share // tile) + index * steps + j)
    in_specs = [whole(us.shape), whole(ut.shape), whole(flipped.shape)]
    in_specs += [pl.BlockSpec((width, tile), column)] * 2 + [pl.BlockSpec((1, tile), column)]
    in_specs += [whole(stats[0].shape)] * groups
    args = [us, ut, flipped, ws, wt, centre, *stats]
    if not first:
        in_specs += [whole(carry[0].shape), whole(carry[1].shape)]
        args += list(carry)
    out_specs = [pl.BlockSpec((slab, tile), lambda j, place_ref: (0, j))] * groups
    out_shape = [jax.ShapeDtypeStruct((slab, chunk), bf16)] * groups
    scratch = [pltpu.VMEM((8, 128), f32)] + [pltpu.VMEM((rows, 128), f32)] * 2
    if last:
        out_specs += [whole((rows // 2, width))] * 2
        out_shape += [jax.ShapeDtypeStruct((rows // 2, width), f32), jax.ShapeDtypeStruct((rows // 2, width), bf16)]
        scratch = [pltpu.VMEM((rows, width), f32)] + scratch
    else:
        out_specs += [whole((rows, width))]
        out_shape += [jax.ShapeDtypeStruct((rows, width), f32)]
    out_specs += [whole((8, 128))]
    out_shape += [jax.ShapeDtypeStruct((8, 128), f32)]
    return pl.pallas_call(
        functools.partial(second_kernel, groups=groups, first=first, last=last, count=count),
        grid_spec=pltpu.PrefetchScalarGridSpec(
            num_scalar_prefetch=1, grid=(steps,), in_specs=in_specs, out_specs=out_specs, scratch_shapes=scratch
        ),
        out_shape=out_shape,
        compiler_params=params(),
        cost_estimate=pl.CostEstimate(flops=8 * rows * width * chunk, bytes_accessed=8 * width * chunk, transcendentals=2 * rows * chunk),
        name="second_pass",
    )(place, *args)


def pieces(value):
    rows = lax.broadcasted_iota(jnp.int32, (PAD, 256), 0)
    out = jnp.zeros((PAD, 256), f32)
    for k in range(3):
        piece = value.astype(bf16).astype(f32)
        out = jnp.where(rows == k, piece, out)
        value = value - piece
    return out.astype(bf16)


def joined(block):
    return jnp.sum(block[:, 0:1].astype(f32), axis=0, keepdims=True)


def core_sum_kernel(keep_ref, got_ref, loss_ref, other_ref, *outs, blocks):
    size = keep_ref.shape[0] // blocks
    loss = loss_ref[0:1, 0:1] + other_ref[0:1, 0:1]
    for k in range(blocks):
        at = slice(k * size, (k + 1) * size)
        outs[k][0:size, :] = (keep_ref[at, :] + got_ref[at, :].astype(f32)).astype(outs[k].dtype)
        if k:
            outs[k][size:, :] = pieces(loss)
    outs[-1][...] = jnp.broadcast_to(loss, outs[-1].shape)


def core_sum(keep, got, loss, other, blocks):
    rows, width = keep.shape
    size = rows // blocks
    return pl.pallas_call(
        functools.partial(core_sum_kernel, blocks=blocks),
        out_shape=[jax.ShapeDtypeStruct((size, width), f32)]
        + [jax.ShapeDtypeStruct((size + PAD, width), bf16)] * (blocks - 1)
        + [jax.ShapeDtypeStruct((8, 128), f32)],
        compiler_params=params(),
        name="core_sum",
    )(keep, got, loss, other)


def axis_sum_kernel(keep_ref, loss_ref, *refs, blocks, sources):
    got, outs = refs[:sources], refs[sources:]
    rows = keep_ref.shape[0]
    size = rows // blocks
    loss = loss_ref[0:1, 0:1]
    for ref in got:
        loss = loss + joined(ref[rows:, :])
    for k in range(blocks):
        at = slice(k * size, (k + 1) * size)
        total = keep_ref[at, :]
        for ref in got:
            total = total + ref[at, :].astype(f32)
        outs[k][0:size, :] = total.astype(outs[k].dtype)
        if k:
            outs[k][size:, :] = pieces(loss)
    outs[-1][...] = jnp.broadcast_to(loss, outs[-1].shape)


def axis_sum(keep, loss, got, blocks):
    rows, width = keep.shape
    size = rows // blocks
    return pl.pallas_call(
        functools.partial(axis_sum_kernel, blocks=blocks, sources=len(got)),
        out_shape=[jax.ShapeDtypeStruct((size, width), f32)]
        + [jax.ShapeDtypeStruct((size + PAD, width), bf16)] * (blocks - 1)
        + [jax.ShapeDtypeStruct((8, 128), f32)],
        compiler_params=params(),
        name="axis_sum",
    )(keep, loss, *got)


def row_kernel(keep_ref, loss_ref, raw_ref, inv_ref, *refs, sources, rows_total):
    got, (out_ref, total_ref) = refs[:sources], refs[sources:]
    rows = keep_ref.shape[0]
    loss = loss_ref[0:1, 0:1]
    grad = keep_ref[...]
    for ref in got:
        loss = loss + joined(ref[rows:, :])
        grad = grad + ref[0:rows, :].astype(f32)
    raw = raw_ref[...]
    inv = inv_ref[:, 0:1]
    out_ref[...] = inv * grad - inv * inv * inv * raw * jnp.sum(raw * grad, axis=-1, keepdims=True)
    total_ref[...] = jnp.broadcast_to(loss / rows_total, total_ref.shape)


def step_kernel(place_ref, *refs, groups):
    grads = refs[:groups]
    student_ref, teacher_ref, first_ref, second_ref = refs[groups : groups + 4]
    out_student, out_first, out_second, out_teacher = refs[-4:]
    source = pl.program_id(0)
    for k in range(groups):

        @pl.when(source == k)
        def _(k=k):
            grad = grads[k][...].astype(f32)
            first = beta_one * first_ref[...] + (1.0 - beta_one) * grad
            second = beta_two * second_ref[...] + (1.0 - beta_two) * grad * grad
            step = first / fix_one / (jnp.sqrt(second / fix_two) + 1e-08)
            student = student_ref[...]
            student = student - learn_rate * (step + decay_rate * student)
            out_student[...] = student
            out_first[...] = first
            out_second[...] = second
            out_teacher[...] = teacher_keep * teacher_ref[...] + (1.0 - teacher_keep) * student


def optimizer(place, grads, student, teacher, first, second, done, index, chunks, share):
    groups = len(grads)
    slab, total = first.shape
    chunk = share // chunks
    tile = min(chunk, 2048)
    steps = chunk // tile
    column = lambda k, j, place_ref: (place_ref[0] ^ k) * (share // tile) + index * steps + j
    sliced = pl.BlockSpec((slab, tile), lambda k, j, place_ref: (place_ref[0], column(k, j, place_ref)))
    local = pl.BlockSpec((slab, tile), lambda k, j, place_ref: (0, column(k, j, place_ref)))
    grad_specs = [
        pl.BlockSpec((slab, tile), lambda k, j, place_ref, g=g: (0, jnp.where(k == g, j, jnp.where(k < g, 0, steps - 1))))
        for g in range(groups)
    ]
    in_specs = grad_specs + [sliced, sliced, local, local]
    args = [*grads, student, teacher, first, second]
    aliases = {}
    if done is not None:
        aliases = {1 + len(args) + i: i for i in range(4)}
        in_specs += [pl.BlockSpec(memory_space=pl.ANY)] * 4
        args += list(done)
    return pl.pallas_call(
        functools.partial(step_kernel, groups=groups),
        grid_spec=pltpu.PrefetchScalarGridSpec(
            num_scalar_prefetch=1, grid=(groups, steps), in_specs=in_specs, out_specs=[local] * 4
        ),
        out_shape=[jax.ShapeDtypeStruct((slab, total), f32)] * 4,
        input_output_aliases=aliases,
        compiler_params=params(),
        cost_estimate=pl.CostEstimate(flops=20 * slab * groups * chunk, bytes_accessed=34 * slab * groups * chunk, transcendentals=0),
        name="optimizer",
    )(place, *args)


def local(
    student_patch,
    teacher_patch,
    patch_image,
    masked_rows,
    student_proto,
    teacher_proto,
    first_moment,
    second_moment,
    centre,
):
    count = masked_rows.shape[1]
    patches, width = student_patch.shape[1:]
    protos = lax.axis_size("proto")
    groups = lax.axis_size("dp")
    columns = student_proto.shape[1]
    share = columns // groups
    images = patches * protos // PATCH_IMG
    ratio = count * PATCH_IMG / patches
    rows_total = count * protos * groups
    place = lax.axis_index("dp").astype(jnp.int32).reshape(1)
    centre = centre.reshape(1, columns)

    def proto_swap(x, k):
        return lax.ppermute(x, "proto", xor_pairs(protos, k))

    def dp_swap(x, k):
        return lax.ppermute(x, "dp", xor_pairs(groups, k))

    pack, raw, inv = pick_rows(masked_rows, patch_image, student_patch[0], teacher_patch[0])
    own = jnp.concatenate([pack] + [proto_swap(pack, k) for k in range(2, protos, 2)], axis=0)
    other = proto_swap(own, 1)
    far = [dp_swap(own, k) for k in range(1, groups)]

    stats = first_pass(own, other, student_proto, teacher_proto, centre, count)
    far_other = [proto_swap(x, 1) for x in far]
    packs = [own, other]
    for pair in zip(far, far_other):
        packs += list(pair)
    us, ut, flipped = lay_rows(place, packs, count)

    rows = stats.shape[1]
    stats = pl.pallas_call(
        core_join_kernel, out_shape=jax.ShapeDtypeStruct(stats.shape, f32), compiler_params=params(), name="core_join"
    )(stats, proto_swap(stats, 1))
    stats, loss_own = pl.pallas_call(
        functools.partial(final_join_kernel, count=count, images=images, ratio=ratio),
        out_shape=[jax.ShapeDtypeStruct(stats.shape, f32), jax.ShapeDtypeStruct((8, 128), f32)],
        compiler_params=params(),
        name="final_join",
    )(stats, *[proto_swap(stats, k) for k in range(2, protos, 2)], own, other)
    all_stats = [stats] + [dp_swap(stats, k) for k in range(1, groups)]

    carry = None
    sent = []
    for index in range(CHUNKS):
        out = second_pass(
            place, us, ut, flipped, student_proto, teacher_proto, centre, all_stats, carry, index, CHUNKS, share, count
        )
        grads, carry = out[:groups], out[groups:]
        sent.append([grads[0]] + [dp_swap(grads[k], k) for k in range(1, groups)])
    keep, send, cross = carry
    loss = loss_own - cross

    zs_count = protos // 2
    out = core_sum(keep, proto_swap(send, 1), loss, proto_swap(loss, 1), zs_count)
    out = axis_sum(out[0], out[-1], [proto_swap(out[k], 2 * k) for k in range(1, zs_count)], groups)
    got = [dp_swap(out[k], k) for k in range(1, groups)]
    row_grad, total = pl.pallas_call(
        functools.partial(row_kernel, sources=len(got), rows_total=rows_total),
        out_shape=[jax.ShapeDtypeStruct((count, width), f32), jax.ShapeDtypeStruct((8, 128), f32)],
        compiler_params=params(),
        name="row_grad",
    )(out[0], out[-1], raw, inv, *got)

    done = None
    for index in range(CHUNKS):
        done = optimizer(
            place, sent[index], student_proto, teacher_proto, first_moment, second_moment, done, index, CHUNKS, share
        )
    new_student, new_first, new_second, new_teacher = done
    return (row_grad[None], new_student, new_first, new_second, new_teacher, total[0, 0])


def solution(mesh):
    in_specs = (
        P("dp", "proto", None),
        P("dp", "proto", None),
        P("dp", "proto"),
        P("dp", "proto"),
        P(None, "proto"),
        P(None, "proto"),
        P("dp", "proto"),
        P("dp", "proto"),
        P("proto"),
    )
    out_specs = (
        P("dp", "proto", None),
        P("dp", "proto"),
        P("dp", "proto"),
        P("dp", "proto"),
        P("dp", "proto"),
        P(),
    )
    return jax.shard_map(local, mesh=mesh, in_specs=in_specs, out_specs=out_specs, check_vma=False)
```

```python
import functools

import jax
import jax.numpy as jnp
from jax import lax
from jax.experimental import pallas as pl
from jax.experimental.pallas import tpu as pltpu
from jax.sharding import PartitionSpec as P

PATCH_IMG = 256

student_temp = 0.1
teacher_temp = 0.07
beta_one = 0.9
beta_two = 0.999
fix_one = 0.9999734386011124
fix_two = 0.09520785288629038
learn_rate = 0.002
decay_rate = 0.04
teacher_keep = 0.994

log2_e = 1.4426950408889634
ln_2 = 0.6931471805599453
scale_s = log2_e / student_temp
scale_t = log2_e / teacher_temp

f32 = jnp.float32
bf16 = jnp.bfloat16
PAD = 16
CHUNKS = 2


def params(mebibytes):
    return pltpu.CompilerParams(vmem_limit_bytes=mebibytes << 20)


def cost(flops, moved):
    return pl.CostEstimate(flops=flops, bytes_accessed=moved, transcendentals=0)


def whole(shape):
    return pl.BlockSpec(shape, lambda *_: (0,) * len(shape))


def xor_pairs(size, k):
    return [(i, i ^ k) for i in range(size)]


def pick_kernel(rows_ref, image_ref, student_ref, teacher_ref, pack_ref, raw_ref, inv_ref):
    patches, width = student_ref.shape
    count = rows_ref.shape[1]
    hot = lax.broadcasted_iota(jnp.int32, (patches, count), 0) == rows_ref[...]
    hot = jnp.where(hot, 1.0, 0.0).astype(bf16)

    def pick(table):
        return lax.dot_general(hot, table, (((0,), (0,)), ((), ())), preferred_element_type=f32)

    def unit(raw):
        inverse = lax.rsqrt(jnp.sum(raw * raw, axis=-1, keepdims=True) + 1e-06)
        return raw * inverse, inverse

    raw_s = pick(student_ref[...])
    unit_s, inv_s = unit(raw_s)
    unit_t, _ = unit(pick(teacher_ref[...]))
    raw_ref[...] = raw_s
    inv_ref[...] = jnp.broadcast_to(inv_s, inv_ref.shape)
    pack_ref[0:count, :] = unit_s.astype(bf16)
    pack_ref[count : 2 * count, :] = unit_t.astype(bf16)
    images = jnp.broadcast_to(image_ref[...].astype(f32), (PAD, patches)).astype(bf16)
    ids = jnp.dot(images, hot, preferred_element_type=f32)
    pack_ref[2 * count :, :] = jnp.zeros((PAD, width), bf16)
    pack_ref[2 * count :, 0:count] = ids.astype(bf16)


def pick_rows(rows, image, student, teacher):
    patches, width = student.shape
    count = rows.shape[1]
    return pl.pallas_call(
        pick_kernel,
        out_shape=[
            jax.ShapeDtypeStruct((2 * count + PAD, width), bf16),
            jax.ShapeDtypeStruct((count, width), f32),
            jax.ShapeDtypeStruct((count, 128), f32),
        ],
        compiler_params=params(8),
        cost_estimate=cost(0, 1 << 20),
        name="pick_rows",
    )(rows, image, student, teacher)


def first_kernel(own_ref, other_ref, ws_ref, wt_ref, centre_ref, out_ref, us, ut, ms, ss, mt, st, *, count):
    step = pl.program_id(0)
    pack = 2 * count + PAD
    rows = us.shape[0]
    half = rows // 2
    cols = ws_ref.shape[1]

    @pl.when(step == 0)
    def _():
        for c, ref in enumerate((own_ref, other_ref)):
            for z in range(half // count):
                at = c * half + z * count
                us[at : at + count, :] = ref[z * pack : z * pack + count, :]
                ut[at : at + count, :] = ref[z * pack + count : z * pack + 2 * count, :]
        for m, s in ((ms, ss), (mt, st)):
            m[...] = jnp.full_like(m, -jnp.inf)
            s[...] = jnp.zeros_like(s)

    def update(parts, m_ref, s_ref, at):
        old = m_ref[at, :]
        new = functools.reduce(jnp.maximum, parts, old)
        total = functools.reduce(jnp.add, [jnp.exp2(part - new) for part in parts])
        s_ref[at, :] = s_ref[at, :] * jnp.exp2(old - new) + total
        m_ref[at, :] = new

    block = min(rows, 512)
    tile = min(cols, 1024)
    for t in range(cols // tile):
        span = slice(t * tile, (t + 1) * tile)
        ws = ws_ref[:, span].astype(bf16)
        wt = wt_ref[:, span].astype(bf16)
        shift = centre_ref[:, span] * scale_t
        for r in range(rows // block):
            at = slice(r * block, (r + 1) * block)
            zs = jnp.dot(us[at, :], ws, preferred_element_type=f32)
            update([zs[:, i : i + 128] * scale_s for i in range(0, tile, 128)], ms, ss, at)
            zt = jnp.dot(ut[at, :], wt, preferred_element_type=f32)
            update([zt[:, i : i + 128] * scale_t - shift[:, i : i + 128] for i in range(0, tile, 128)], mt, st, at)

    @pl.when(step == pl.num_programs(0) - 1)
    def _():
        out_ref[...] = jnp.zeros_like(out_ref)
        for k, (m, s) in enumerate(((ms, ss), (mt, st))):
            lanes = m[...]
            peak = jnp.max(lanes, axis=1, keepdims=True)
            total = jnp.sum(s[...] * jnp.exp2(lanes - peak), axis=1, keepdims=True)
            lse = jnp.broadcast_to(peak + jnp.log2(total), lanes.shape)
            out_ref[k : k + 1, :] = jnp.transpose(lse)[0:1, :]


def first_pass(own, other, ws, wt, centre, count):
    width, cols = ws.shape
    rows = 2 * own.shape[0] // (2 * count + PAD) * count
    tile = min(cols, 2048)
    return pl.pallas_call(
        functools.partial(first_kernel, count=count),
        grid=(cols // tile,),
        in_specs=[
            whole(own.shape),
            whole(other.shape),
            pl.BlockSpec((width, tile), lambda j: (0, j)),
            pl.BlockSpec((width, tile), lambda j: (0, j)),
            pl.BlockSpec((1, tile), lambda j: (0, j)),
        ],
        out_specs=whole((8, rows)),
        out_shape=jax.ShapeDtypeStruct((8, rows), f32),
        scratch_shapes=[pltpu.VMEM((rows, width), bf16)] * 2 + [pltpu.VMEM((rows, 128), f32)] * 4,
        compiler_params=params(24),
        cost_estimate=cost(4 * rows * width * cols, 8 * width * cols),
        name="first_pass",
    )(own, other, ws, wt, centre)


def join(parts):
    peak = functools.reduce(jnp.maximum, parts)
    total = functools.reduce(jnp.add, [jnp.exp2(part - peak) for part in parts])
    return peak + jnp.log2(total)


def swap_blocks(x, k, size):
    n = x.shape[1] // size
    return jnp.concatenate([x[:, (j ^ k) * size : ((j ^ k) + 1) * size] for j in range(n)], axis=1)


def core_join_kernel(own_ref, other_ref, out_ref):
    half = own_ref.shape[1] // 2
    out_ref[...] = join([own_ref[...], swap_blocks(other_ref[...], 1, half)])


def final_join_kernel(*refs, count, images, ratio):
    stats, (own_ref, other_ref), (out_ref, loss_ref) = refs[:-4], refs[-4:-2], refs[-2:]
    rows = stats[0].shape[1]
    pack = 2 * count + PAD
    lse = join([swap_blocks(ref[...], k, count) for k, ref in enumerate(stats)])
    ids = jnp.concatenate(
        [
            ref[z * pack + 2 * count : (z + 1) * pack, 0:count].astype(f32)[0:8, :]
            for ref in (own_ref, other_ref)
            for z in range(rows // (2 * count))
        ],
        axis=1,
    )
    per_row = jnp.zeros_like(ids)
    for label in range(images):
        match = jnp.where(ids == label, 1.0, 0.0)
        per_row += match * jnp.sum(match, axis=1, keepdims=True)
    weight = ratio / per_row
    out_ref[...] = lse - jnp.log2(weight / student_temp)
    own = jnp.sum(weight[0:1, 0:count] * lse[0:1, 0:count] * ln_2, axis=1, keepdims=True)
    loss_ref[...] = jnp.broadcast_to(own, loss_ref.shape)


def lay_kernel(slab_ref, *refs, count, groups):
    packs, us, ut, flipped, turned = refs[: 2 * groups], refs[-4], refs[-3], refs[-2], refs[-1]
    pack = 2 * count + PAD
    zs = packs[0].shape[0] // pack
    at = 0
    for g in range(groups):
        for c in range(2):
            ref = packs[2 * g + c]
            for z in range(zs):
                us[at : at + count, :] = ref[z * pack : z * pack + count, :]
                ut[at : at + count, :] = ref[z * pack + count : z * pack + 2 * count, :]
                at += count
    width = us.shape[1]
    turned[...] = jnp.transpose(us[...])
    slab = width // groups
    for k in range(groups):
        start = pl.multiple_of((slab_ref[0] ^ k) * slab, slab)
        flipped[k * slab : (k + 1) * slab, :] = turned[pl.ds(start, slab), :]


def lay_rows(slab, packs, count):
    groups = len(packs) // 2
    width = packs[0].shape[1]
    rows = 2 * groups * (packs[0].shape[0] // (2 * count + PAD)) * count
    return pl.pallas_call(
        functools.partial(lay_kernel, count=count, groups=groups),
        in_specs=[pl.BlockSpec(memory_space=pltpu.SMEM)] + [pl.BlockSpec(memory_space=pltpu.VMEM)] * len(packs),
        out_shape=[jax.ShapeDtypeStruct((rows, width), bf16)] * 2 + [jax.ShapeDtypeStruct((width, rows), bf16)],
        scratch_shapes=[pltpu.VMEM((width, rows), bf16)],
        compiler_params=params(16),
        cost_estimate=cost(0, 4 << 20),
        name="lay_rows",
    )(slab, *packs)


def second_kernel(place_ref, us, ut, flipped, ws_ref, wt_ref, centre_ref, *refs, groups, first, last, count):
    stats = refs[:groups]
    refs = refs[groups:]
    if first:
        carry_ref = seed_ref = None
    else:
        carry_ref, seed_ref = refs[:2]
        refs = refs[2:]
    grads, refs = refs[:groups], refs[groups:]
    if last:
        keep_ref, send_ref, loss_ref, total, loss_sum, shift_s, shift_t = refs
    else:
        total, loss_ref, loss_sum, shift_s, shift_t = refs
    step = pl.program_id(0)
    rows, width = us.shape
    group_rows = rows // groups
    tile = ws_ref.shape[1]

    @pl.when(step == 0)
    def _():
        total[...] = jnp.zeros_like(total) if first else carry_ref[...]
        loss_sum[...] = jnp.zeros_like(loss_sum)
        for g in range(groups):
            at = slice(g * group_rows, (g + 1) * group_rows)
            for k, shift in enumerate((shift_s, shift_t)):
                line = jnp.broadcast_to(stats[g][k : k + 1, :], (128, group_rows))
                shift[at, :] = jnp.transpose(line)

    ws = ws_ref[...].astype(bf16)
    wt = wt_ref[...].astype(bf16)
    centre = centre_ref[...] * scale_t
    block = min(group_rows, 512)
    grad = None
    for r in range(rows // block):
        at = slice(r * block, (r + 1) * block)
        zs = jnp.dot(us[at, :], ws, preferred_element_type=f32)
        zt = jnp.dot(ut[at, :], wt, preferred_element_type=f32)
        as_, at_ = shift_s[at, :], shift_t[at, :]
        parts = []
        loss = None
        for i in range(0, tile, 128):
            zsi = zs[:, i : i + 128]
            ps = jnp.exp2(zsi * scale_s - as_)
            pt = jnp.exp2(zt[:, i : i + 128] * scale_t - centre[:, i : i + 128] - at_)
            cross = pt * zsi
            loss = cross if loss is None else loss + cross
            parts.append((ps - pt).astype(bf16))
        loss_sum[...] += jnp.sum(loss.reshape(block // 8, 8, 128), axis=0)
        logit = jnp.concatenate(parts, axis=1)
        total[at, :] += lax.dot_general(logit, ws, (((1,), (1,)), ((), ())), preferred_element_type=f32)
        part = jnp.dot(flipped[:, at], logit, preferred_element_type=f32)
        grad = part if grad is None else grad + part
    slab = width // groups
    for k in range(groups):
        grads[k][...] = grad[k * slab : (k + 1) * slab, :].astype(bf16)

    @pl.when(step == pl.num_programs(0) - 1)
    def _():
        done = jnp.sum(jnp.sum(loss_sum[...], axis=1, keepdims=True), axis=0, keepdims=True)
        loss = jnp.broadcast_to(done, loss_ref.shape)
        if not first:
            loss += seed_ref[...]
        loss_ref[...] = loss
        if last:
            zs_count = group_rows // (2 * count)
            for g in range(groups):
                for c, ref in enumerate((keep_ref, send_ref)):
                    for z in range(zs_count):
                        src = g * group_rows + (c * zs_count + z) * count
                        dst = (z * groups + g) * count
                        ref[dst : dst + count, :] = total[src : src + count, :].astype(ref.dtype)


def second_pass(place, us, ut, flipped, ws, wt, centre, stats, carry, index, chunks, share, count):
    rows, width = us.shape
    groups = len(stats)
    slab = width // groups
    chunk = share // chunks
    tile = min(chunk, 512)
    steps = chunk // tile
    first, last = index == 0, index == chunks - 1
    column = lambda j, place_ref: (0, place_ref[0] * (share // tile) + index * steps + j)
    in_specs = [whole(us.shape), whole(ut.shape), whole(flipped.shape)]
    in_specs += [pl.BlockSpec((width, tile), column)] * 2 + [pl.BlockSpec((1, tile), column)]
    in_specs += [whole(stats[0].shape)] * groups
    args = [us, ut, flipped, ws, wt, centre, *stats]
    if not first:
        in_specs += [whole(carry[0].shape), whole(carry[1].shape)]
        args += list(carry)
    out_specs = [pl.BlockSpec((slab, tile), lambda j, place_ref: (0, j))] * groups
    out_shape = [jax.ShapeDtypeStruct((slab, chunk), bf16)] * groups
    scratch = [pltpu.VMEM((8, 128), f32)] + [pltpu.VMEM((rows, 128), f32)] * 2
    if last:
        out_specs += [whole((rows // 2, width))] * 2
        out_shape += [jax.ShapeDtypeStruct((rows // 2, width), f32), jax.ShapeDtypeStruct((rows // 2, width), bf16)]
        scratch = [pltpu.VMEM((rows, width), f32)] + scratch
    else:
        out_specs += [whole((rows, width))]
        out_shape += [jax.ShapeDtypeStruct((rows, width), f32)]
    out_specs += [whole((8, 128))]
    out_shape += [jax.ShapeDtypeStruct((8, 128), f32)]
    return pl.pallas_call(
        functools.partial(second_kernel, groups=groups, first=first, last=last, count=count),
        grid_spec=pltpu.PrefetchScalarGridSpec(
            num_scalar_prefetch=1, grid=(steps,), in_specs=in_specs, out_specs=out_specs, scratch_shapes=scratch
        ),
        out_shape=out_shape,
        compiler_params=params(32),
        cost_estimate=cost(8 * rows * width * chunk, 8 * width * chunk),
        name="second_pass",
    )(place, *args)


def pieces(value):
    rows = lax.broadcasted_iota(jnp.int32, (PAD, 256), 0)
    out = jnp.zeros((PAD, 256), f32)
    for k in range(3):
        piece = value.astype(bf16).astype(f32)
        out = jnp.where(rows == k, piece, out)
        value = value - piece
    return out.astype(bf16)


def joined(block):
    return jnp.sum(block[:, 0:1].astype(f32), axis=0, keepdims=True)


def core_sum_kernel(keep_ref, got_ref, loss_ref, other_ref, *outs, blocks):
    size = keep_ref.shape[0] // blocks
    loss = loss_ref[0:1, 0:1] + other_ref[0:1, 0:1]
    for k in range(blocks):
        at = slice(k * size, (k + 1) * size)
        outs[k][0:size, :] = (keep_ref[at, :] + got_ref[at, :].astype(f32)).astype(outs[k].dtype)
        if k:
            outs[k][size:, :] = pieces(loss)
    outs[-1][...] = jnp.broadcast_to(loss, outs[-1].shape)


def core_sum(keep, got, loss, other, blocks):
    rows, width = keep.shape
    size = rows // blocks
    return pl.pallas_call(
        functools.partial(core_sum_kernel, blocks=blocks),
        out_shape=[jax.ShapeDtypeStruct((size, width), f32)]
        + [jax.ShapeDtypeStruct((size + PAD, width), bf16)] * (blocks - 1)
        + [jax.ShapeDtypeStruct((8, 128), f32)],
        compiler_params=params(8),
        cost_estimate=cost(0, 1 << 20),
        name="core_sum",
    )(keep, got, loss, other)


def axis_sum_kernel(keep_ref, loss_ref, *refs, blocks, sources):
    got, outs = refs[:sources], refs[sources:]
    rows = keep_ref.shape[0]
    size = rows // blocks
    loss = loss_ref[0:1, 0:1]
    for ref in got:
        loss = loss + joined(ref[rows:, :])
    for k in range(blocks):
        at = slice(k * size, (k + 1) * size)
        total = keep_ref[at, :]
        for ref in got:
            total = total + ref[at, :].astype(f32)
        outs[k][0:size, :] = total.astype(outs[k].dtype)
        if k:
            outs[k][size:, :] = pieces(loss)
    outs[-1][...] = jnp.broadcast_to(loss, outs[-1].shape)


def axis_sum(keep, loss, got, blocks):
    rows, width = keep.shape
    size = rows // blocks
    return pl.pallas_call(
        functools.partial(axis_sum_kernel, blocks=blocks, sources=len(got)),
        out_shape=[jax.ShapeDtypeStruct((size, width), f32)]
        + [jax.ShapeDtypeStruct((size + PAD, width), bf16)] * (blocks - 1)
        + [jax.ShapeDtypeStruct((8, 128), f32)],
        compiler_params=params(8),
        cost_estimate=cost(0, 1 << 20),
        name="axis_sum",
    )(keep, loss, *got)


def row_kernel(keep_ref, loss_ref, raw_ref, inv_ref, *refs, sources, rows_total):
    got, (out_ref, total_ref) = refs[:sources], refs[sources:]
    rows = keep_ref.shape[0]
    loss = loss_ref[0:1, 0:1]
    grad = keep_ref[...]
    for ref in got:
        loss = loss + joined(ref[rows:, :])
        grad = grad + ref[0:rows, :].astype(f32)
    raw = raw_ref[...]
    inv = inv_ref[:, 0:1]
    out_ref[...] = inv * grad - inv * inv * inv * raw * jnp.sum(raw * grad, axis=-1, keepdims=True)
    total_ref[...] = jnp.broadcast_to(loss / rows_total, total_ref.shape)


def step_kernel(place_ref, *refs, groups):
    grads = refs[:groups]
    student_ref, teacher_ref, first_ref, second_ref = refs[groups : groups + 4]
    out_student, out_first, out_second, out_teacher = refs[-4:]
    source = pl.program_id(0)
    for k in range(groups):

        @pl.when(source == k)
        def _(k=k):
            grad = grads[k][...].astype(f32)
            first = beta_one * first_ref[...] + (1.0 - beta_one) * grad
            second = beta_two * second_ref[...] + (1.0 - beta_two) * grad * grad
            step = first / fix_one / (jnp.sqrt(second / fix_two) + 1e-08)
            student = student_ref[...]
            student = student - learn_rate * (step + decay_rate * student)
            out_student[...] = student
            out_first[...] = first
            out_second[...] = second
            out_teacher[...] = teacher_keep * teacher_ref[...] + (1.0 - teacher_keep) * student


def optimizer(place, grads, student, teacher, first, second, done, index, chunks, share):
    groups = len(grads)
    slab, total = first.shape
    chunk = share // chunks
    tile = min(chunk, 2048)
    steps = chunk // tile
    column = lambda k, j, place_ref: (place_ref[0] ^ k) * (share // tile) + index * steps + j
    sliced = pl.BlockSpec((slab, tile), lambda k, j, place_ref: (place_ref[0], column(k, j, place_ref)))
    local = pl.BlockSpec((slab, tile), lambda k, j, place_ref: (0, column(k, j, place_ref)))
    grad_specs = [
        pl.BlockSpec((slab, tile), lambda k, j, place_ref, g=g: (0, jnp.where(k == g, j, jnp.where(k < g, 0, steps - 1))))
        for g in range(groups)
    ]
    in_specs = grad_specs + [sliced, sliced, local, local]
    args = [*grads, student, teacher, first, second]
    aliases = {}
    if done is not None:
        aliases = {1 + len(args) + i: i for i in range(4)}
        in_specs += [pl.BlockSpec(memory_space=pl.ANY)] * 4
        args += list(done)
    return pl.pallas_call(
        functools.partial(step_kernel, groups=groups),
        grid_spec=pltpu.PrefetchScalarGridSpec(
            num_scalar_prefetch=1, grid=(groups, steps), in_specs=in_specs, out_specs=[local] * 4
        ),
        out_shape=[jax.ShapeDtypeStruct((slab, total), f32)] * 4,
        input_output_aliases=aliases,
        compiler_params=params(16),
        cost_estimate=cost(20 * slab * groups * chunk, 34 * slab * groups * chunk),
        name="optimizer",
    )(place, *args)


def local(
    student_patch,
    teacher_patch,
    patch_image,
    masked_rows,
    student_proto,
    teacher_proto,
    first_moment,
    second_moment,
    centre,
):
    count = masked_rows.shape[1]
    patches, width = student_patch.shape[1:]
    protos = lax.axis_size("proto")
    groups = lax.axis_size("dp")
    columns = student_proto.shape[1]
    share = columns // groups
    images = patches * protos // PATCH_IMG
    ratio = count * PATCH_IMG / patches
    rows_total = count * protos * groups
    place = lax.axis_index("dp").astype(jnp.int32).reshape(1)
    centre = centre.reshape(1, columns)

    def proto_swap(x, k):
        return lax.ppermute(x, "proto", xor_pairs(protos, k))

    def dp_swap(x, k):
        return lax.ppermute(x, "dp", xor_pairs(groups, k))

    pack, raw, inv = pick_rows(masked_rows, patch_image, student_patch[0], teacher_patch[0])
    own = jnp.concatenate([pack] + [proto_swap(pack, k) for k in range(2, protos, 2)], axis=0)
    other = proto_swap(own, 1)
    far = [dp_swap(own, k) for k in range(1, groups)]

    stats = first_pass(own, other, student_proto, teacher_proto, centre, count)
    stats, *far = lax.optimization_barrier((stats, *far))
    far_other = [proto_swap(x, 1) for x in far]
    packs = [own, other]
    for pair in zip(far, far_other):
        packs += list(pair)
    us, ut, flipped = lay_rows(place, packs, count)

    stats = pl.pallas_call(
        core_join_kernel,
        out_shape=jax.ShapeDtypeStruct(stats.shape, f32),
        compiler_params=params(8),
        cost_estimate=cost(0, 1 << 20),
        name="core_join",
    )(stats, proto_swap(stats, 1))
    stats, loss_own = pl.pallas_call(
        functools.partial(final_join_kernel, count=count, images=images, ratio=ratio),
        out_shape=[jax.ShapeDtypeStruct(stats.shape, f32), jax.ShapeDtypeStruct((8, 128), f32)],
        compiler_params=params(8),
        cost_estimate=cost(0, 1 << 20),
        name="final_join",
    )(stats, *[proto_swap(stats, k) for k in range(2, protos, 2)], own, other)
    all_stats = [stats] + [dp_swap(stats, k) for k in range(1, groups)]

    carry = None
    sent = []
    for index in range(CHUNKS):
        out = second_pass(
            place, us, ut, flipped, student_proto, teacher_proto, centre, all_stats, carry, index, CHUNKS, share, count
        )
        grads, carry = out[:groups], out[groups:]
        sent.append([grads[0]] + [dp_swap(grads[k], k) for k in range(1, groups)])
    keep, send, cross = carry
    send, sent[:-1] = lax.optimization_barrier((send, sent[:-1]))
    loss = loss_own - cross

    zs_count = protos // 2
    out = core_sum(keep, proto_swap(send, 1), loss, proto_swap(loss, 1), zs_count)
    out = axis_sum(out[0], out[-1], [proto_swap(out[k], 2 * k) for k in range(1, zs_count)], groups)
    got = [dp_swap(out[k], k) for k in range(1, groups)]
    row_grad, total = pl.pallas_call(
        functools.partial(row_kernel, sources=len(got), rows_total=rows_total),
        out_shape=[jax.ShapeDtypeStruct((count, width), f32), jax.ShapeDtypeStruct((8, 128), f32)],
        compiler_params=params(8),
        cost_estimate=cost(0, 1 << 20),
        name="row_grad",
    )(out[0], out[-1], raw, inv, *got)

    done = None
    for index in range(CHUNKS):
        done = optimizer(
            place, sent[index], student_proto, teacher_proto, first_moment, second_moment, done, index, CHUNKS, share
        )
    new_student, new_first, new_second, new_teacher = done
    return (row_grad[None], new_student, new_first, new_second, new_teacher, total[0, 0])


def solution(mesh):
    in_specs = (
        P("dp", "proto", None),
        P("dp", "proto", None),
        P("dp", "proto"),
        P("dp", "proto"),
        P(None, "proto"),
        P(None, "proto"),
        P("dp", "proto"),
        P("dp", "proto"),
        P("proto"),
    )
    out_specs = (
        P("dp", "proto", None),
        P("dp", "proto"),
        P("dp", "proto"),
        P("dp", "proto"),
        P("dp", "proto"),
        P(),
    )
    return jax.shard_map(local, mesh=mesh, in_specs=in_specs, out_specs=out_specs, check_vma=False)
```

```python
import functools

import jax
import jax.numpy as jnp
from jax import lax
from jax.experimental import pallas as pl
from jax.experimental.pallas import tpu as pltpu
from jax.sharding import PartitionSpec as P

PATCH_IMG = 256

student_temp = 0.1
teacher_temp = 0.07
beta_one = 0.9
beta_two = 0.999
fix_one = 0.9999734386011124
fix_two = 0.09520785288629038
learn_rate = 0.002
decay_rate = 0.04
teacher_keep = 0.994

log2_e = 1.4426950408889634
ln_2 = 0.6931471805599453
least = 2.0**-60
most = 2.0**120
scale_s = log2_e / student_temp
scale_t = log2_e / teacher_temp

f32 = jnp.float32
bf16 = jnp.bfloat16
PAD = 16
CHUNKS = 2


def params(mebibytes):
    return pltpu.CompilerParams(vmem_limit_bytes=mebibytes << 20)


def cost(flops, moved):
    return pl.CostEstimate(flops=flops, bytes_accessed=moved, transcendentals=0)


def whole(shape):
    return pl.BlockSpec(shape, lambda *_: (0,) * len(shape))


def xor_pairs(size, k):
    return [(i, i ^ k) for i in range(size)]


def pick_kernel(rows_ref, image_ref, student_ref, teacher_ref, pack_ref, raw_ref, inv_ref):
    patches, width = student_ref.shape
    count = rows_ref.shape[1]
    hot = lax.broadcasted_iota(jnp.int32, (patches, count), 0) == rows_ref[...]
    hot = jnp.where(hot, 1.0, 0.0).astype(bf16)

    def pick(table):
        return lax.dot_general(hot, table, (((0,), (0,)), ((), ())), preferred_element_type=f32)

    def unit(raw):
        inverse = lax.rsqrt(jnp.sum(raw * raw, axis=-1, keepdims=True) + 1e-06)
        return raw * inverse, inverse

    raw_s = pick(student_ref[...])
    unit_s, inv_s = unit(raw_s)
    unit_t, _ = unit(pick(teacher_ref[...]))
    raw_ref[...] = raw_s
    inv_ref[...] = jnp.broadcast_to(inv_s, inv_ref.shape)
    pack_ref[0:count, :] = unit_s.astype(bf16)
    pack_ref[count : 2 * count, :] = unit_t.astype(bf16)
    images = jnp.broadcast_to(image_ref[...].astype(f32), (PAD, patches)).astype(bf16)
    ids = jnp.dot(images, hot, preferred_element_type=f32)
    pack_ref[2 * count :, :] = jnp.zeros((PAD, width), bf16)
    pack_ref[2 * count :, 0:count] = ids.astype(bf16)


def pick_rows(rows, image, student, teacher):
    patches, width = student.shape
    count = rows.shape[1]
    return pl.pallas_call(
        pick_kernel,
        out_shape=[
            jax.ShapeDtypeStruct((2 * count + PAD, width), bf16),
            jax.ShapeDtypeStruct((count, width), f32),
            jax.ShapeDtypeStruct((count, 128), f32),
        ],
        compiler_params=params(56),
        cost_estimate=cost(0, 1 << 20),
        name="pick_rows",
    )(rows, image, student, teacher)


def round_kernel(s_ref, t_ref, out_s, out_t):
    out_s[...] = s_ref[...].astype(bf16)
    out_t[...] = t_ref[...].astype(bf16)


def round_protos(student, teacher):
    width, cols = student.shape
    tile = min(cols, 2048)
    column = pl.BlockSpec((width, tile), lambda j: (0, j))
    return pl.pallas_call(
        round_kernel,
        grid=(cols // tile,),
        in_specs=[column] * 2,
        out_specs=[column] * 2,
        out_shape=[jax.ShapeDtypeStruct((width, cols), bf16)] * 2,
        compiler_params=params(24),
        cost_estimate=cost(0, 12 * width * cols),
        name="round_protos",
    )(student, teacher)


def first_kernel(own_ref, other_ref, ws_ref, wt_ref, centre_ref, out_ref, us, ut, ms, ss, mt, st, *, count):
    pack = 2 * count + PAD
    rows = us.shape[0]
    half = rows // 2
    cols = ws_ref.shape[1]
    for c, ref in enumerate((own_ref, other_ref)):
        for z in range(half // count):
            at = c * half + z * count
            us[at : at + count, :] = ref[z * pack : z * pack + count, :]
            ut[at : at + count, :] = ref[z * pack + count : z * pack + 2 * count, :]

    block = min(rows, 512)
    tile = min(cols, 1024)
    unroll = 2 if cols % (2 * tile) == 0 else 1

    def sweep(update):
        @pl.loop(0, cols // (tile * unroll))
        def _(j):
            for u in range(unroll):
                span = pl.ds(pl.multiple_of((j * unroll + u) * tile, tile), tile)
                ws = ws_ref[:, span]
                wt = wt_ref[:, span]
                shift = centre_ref[:, span] * scale_t
                for r in range(rows // block):
                    at = slice(r * block, (r + 1) * block)
                    zs = jnp.dot(us[at, :], ws, preferred_element_type=f32)
                    update([zs[:, i : i + 128] * scale_s for i in range(0, tile, 128)], ms, ss, at)
                    zt = jnp.dot(ut[at, :], wt, preferred_element_type=f32)
                    update([zt[:, i : i + 128] * scale_t - shift[:, i : i + 128] for i in range(0, tile, 128)], mt, st, at)

    def plain(parts, m_ref, s_ref, at):
        s_ref[at, :] += functools.reduce(jnp.add, [jnp.exp2(part) for part in parts])

    def running(parts, m_ref, s_ref, at):
        old = m_ref[at, :]
        new = functools.reduce(jnp.maximum, parts, old)
        total = functools.reduce(jnp.add, [jnp.exp2(part - new) for part in parts])
        s_ref[at, :] = s_ref[at, :] * jnp.exp2(old - new) + total
        m_ref[at, :] = new

    for m, s in ((ms, ss), (mt, st)):
        m[...] = jnp.zeros_like(m)
        s[...] = jnp.zeros_like(s)
    sweep(plain)
    far = jnp.zeros((rows, 1), f32)
    for s in (ss, st):
        total = jnp.sum(s[...], axis=1, keepdims=True)
        far = jnp.maximum(far, jnp.where((total > least) & (total < most), 0.0, 1.0))

    @pl.when(jnp.max(far) > 0.5)
    def _():
        for m, s in ((ms, ss), (mt, st)):
            m[...] = jnp.full_like(m, -jnp.inf)
            s[...] = jnp.zeros_like(s)
        sweep(running)

    out_ref[...] = jnp.zeros_like(out_ref)
    for k, (m, s) in enumerate(((ms, ss), (mt, st))):
        lanes = m[...]
        peak = jnp.max(lanes, axis=1, keepdims=True)
        total = jnp.sum(s[...] * jnp.exp2(lanes - peak), axis=1, keepdims=True)
        lse = jnp.broadcast_to(peak + jnp.log2(total), lanes.shape)
        out_ref[k : k + 1, :] = jnp.transpose(lse)[0:1, :]


def first_pass(own, other, ws, wt, centre, count):
    width, cols = ws.shape
    rows = 2 * own.shape[0] // (2 * count + PAD) * count
    return pl.pallas_call(
        functools.partial(first_kernel, count=count),
        in_specs=[pl.BlockSpec(memory_space=pltpu.VMEM)] * 5,
        out_shape=jax.ShapeDtypeStruct((8, rows), f32),
        scratch_shapes=[pltpu.VMEM((rows, width), bf16)] * 2 + [pltpu.VMEM((rows, 128), f32)] * 4,
        compiler_params=params(10),
        cost_estimate=cost(4 * rows * width * cols, 4 * width * cols),
        name="first_pass",
    )(own, other, ws, wt, centre)


def join(parts):
    peak = functools.reduce(jnp.maximum, parts)
    total = functools.reduce(jnp.add, [jnp.exp2(part - peak) for part in parts])
    return peak + jnp.log2(total)


def swap_blocks(x, k, size):
    n = x.shape[1] // size
    return jnp.concatenate([x[:, (j ^ k) * size : ((j ^ k) + 1) * size] for j in range(n)], axis=1)


def core_join_kernel(own_ref, other_ref, out_ref):
    half = own_ref.shape[1] // 2
    out_ref[...] = join([own_ref[...], swap_blocks(other_ref[...], 1, half)])


def final_join_kernel(*refs, count, images, ratio):
    stats, (own_ref, other_ref), (out_ref, loss_ref) = refs[:-4], refs[-4:-2], refs[-2:]
    rows = stats[0].shape[1]
    pack = 2 * count + PAD
    lse = join([swap_blocks(ref[...], k, count) for k, ref in enumerate(stats)])
    ids = jnp.concatenate(
        [
            ref[z * pack + 2 * count : (z + 1) * pack, 0:count].astype(f32)[0:8, :]
            for ref in (own_ref, other_ref)
            for z in range(rows // (2 * count))
        ],
        axis=1,
    )
    per_row = jnp.zeros_like(ids)
    for label in range(images):
        match = jnp.where(ids == label, 1.0, 0.0)
        per_row += match * jnp.sum(match, axis=1, keepdims=True)
    weight = ratio / per_row
    out_ref[...] = lse - jnp.log2(weight / student_temp)
    own = jnp.sum(weight[0:1, 0:count] * lse[0:1, 0:count] * ln_2, axis=1, keepdims=True)
    loss_ref[...] = jnp.broadcast_to(own, loss_ref.shape)


def lay_kernel(slab_ref, *refs, count, groups):
    packs, us, ut, flipped, turned = refs[: 2 * groups], refs[-4], refs[-3], refs[-2], refs[-1]
    pack = 2 * count + PAD
    zs = packs[0].shape[0] // pack
    at = 0
    for g in range(groups):
        for c in range(2):
            ref = packs[2 * g + c]
            for z in range(zs):
                us[at : at + count, :] = ref[z * pack : z * pack + count, :]
                ut[at : at + count, :] = ref[z * pack + count : z * pack + 2 * count, :]
                at += count
    width = us.shape[1]
    turned[...] = jnp.transpose(us[...])
    slab = width // groups
    for k in range(groups):
        start = pl.multiple_of((slab_ref[0] ^ k) * slab, slab)
        flipped[k * slab : (k + 1) * slab, :] = turned[pl.ds(start, slab), :]


def lay_rows(slab, packs, count):
    groups = len(packs) // 2
    width = packs[0].shape[1]
    rows = 2 * groups * (packs[0].shape[0] // (2 * count + PAD)) * count
    return pl.pallas_call(
        functools.partial(lay_kernel, count=count, groups=groups),
        in_specs=[pl.BlockSpec(memory_space=pltpu.SMEM)] + [pl.BlockSpec(memory_space=pltpu.VMEM)] * len(packs),
        out_shape=[jax.ShapeDtypeStruct((rows, width), bf16)] * 2 + [jax.ShapeDtypeStruct((width, rows), bf16)],
        scratch_shapes=[pltpu.VMEM((width, rows), bf16)],
        compiler_params=params(16),
        cost_estimate=cost(0, 4 << 20),
        name="lay_rows",
    )(slab, *packs)


def second_kernel(us, ut, flipped, ws_ref, wt_ref, centre_ref, *refs, groups, index, chunk, last, count):
    stats, refs = refs[:groups], refs[groups:]
    if index:
        (carry_ref, seed_ref), refs = refs[:2], refs[2:]
    grads, refs = refs[:groups], refs[groups:]
    if last:
        keep_ref, send_ref, loss_ref, total, loss_sum, shift_s, shift_t = refs
    else:
        total, loss_ref, loss_sum, shift_s, shift_t = refs
    rows, width = us.shape
    group_rows = rows // groups
    slab = width // groups
    total[...] = carry_ref[...] if index else jnp.zeros_like(total)
    loss_sum[...] = jnp.zeros_like(loss_sum)
    for g in range(groups):
        at = slice(g * group_rows, (g + 1) * group_rows)
        for k, shift in enumerate((shift_s, shift_t)):
            shift[at, :] = jnp.transpose(jnp.broadcast_to(stats[g][k : k + 1, :], (128, group_rows)))

    tile = min(chunk, 512)
    block = min(group_rows, 256)
    places = [slice(r * block, (r + 1) * block) for r in range(rows // block)]

    @pl.loop(0, chunk // tile)
    def _(j):
        span = pl.ds(pl.multiple_of(index * chunk + j * tile, tile), tile)
        ws = ws_ref[:, span]
        wt = wt_ref[:, span]
        centre = centre_ref[:, span] * scale_t

        def products(at):
            return (
                jnp.dot(us[at, :], ws, preferred_element_type=f32),
                jnp.dot(ut[at, :], wt, preferred_element_type=f32),
            )

        ready = products(places[0])
        grad = None
        for r, at in enumerate(places):
            zs, zt = ready
            if r + 1 < len(places):
                ready = products(places[r + 1])
            down_s, down_t = shift_s[at, :], shift_t[at, :]
            parts = []
            loss = None
            for i in range(0, tile, 128):
                zsi = zs[:, i : i + 128]
                ps = jnp.exp2(zsi * scale_s - down_s)
                pt = jnp.exp2(zt[:, i : i + 128] * scale_t - centre[:, i : i + 128] - down_t)
                cross = pt * zsi
                loss = cross if loss is None else loss + cross
                parts.append((ps - pt).astype(bf16))
            loss_sum[...] += jnp.sum(loss.reshape(block // 8, 8, 128), axis=0)
            logit = jnp.concatenate(parts, axis=1)
            total[at, :] += lax.dot_general(logit, ws, (((1,), (1,)), ((), ())), preferred_element_type=f32)
            part = jnp.dot(flipped[:, at], logit, preferred_element_type=f32)
            grad = part if grad is None else grad + part
        out = pl.ds(pl.multiple_of(j * tile, tile), tile)
        for k in range(groups):
            grads[k][:, out] = grad[k * slab : (k + 1) * slab, :].astype(bf16)

    done = jnp.sum(jnp.sum(loss_sum[...], axis=1, keepdims=True), axis=0, keepdims=True)
    loss = jnp.broadcast_to(done, loss_ref.shape)
    loss_ref[...] = loss + seed_ref[...] if index else loss
    if last:
        depth = group_rows // (2 * count)
        for g in range(groups):
            for c, ref in enumerate((keep_ref, send_ref)):
                for z in range(depth):
                    src = g * group_rows + (c * depth + z) * count
                    dst = (z * groups + g) * count
                    ref[dst : dst + count, :] = total[src : src + count, :].astype(ref.dtype)


def second_pass(us, ut, flipped, ws, wt, centre, stats, carry, index, chunks, count):
    rows, width = us.shape
    groups = len(stats)
    slab = width // groups
    chunk = ws.shape[1] // chunks
    last = index == chunks - 1
    args = [us, ut, flipped, ws, wt, centre, *stats]
    if index:
        args += list(carry)
    out_shape = [jax.ShapeDtypeStruct((slab, chunk), bf16)] * groups
    scratch = [pltpu.VMEM((8, 128), f32)] + [pltpu.VMEM((rows, 128), f32)] * 2
    if last:
        out_shape += [jax.ShapeDtypeStruct((rows // 2, width), f32), jax.ShapeDtypeStruct((rows // 2, width), bf16)]
        scratch = [pltpu.VMEM((rows, width), f32)] + scratch
    else:
        out_shape += [jax.ShapeDtypeStruct((rows, width), f32)]
    out_shape += [jax.ShapeDtypeStruct((8, 128), f32)]
    held = 2 * rows * 128 * 4 + rows * width * 4
    return pl.pallas_call(
        functools.partial(second_kernel, groups=groups, index=index, chunk=chunk, last=last, count=count),
        in_specs=[pl.BlockSpec(memory_space=pltpu.VMEM)] * len(args),
        out_shape=out_shape,
        scratch_shapes=scratch,
        compiler_params=params((held >> 20) + 8),
        cost_estimate=cost(8 * rows * width * chunk, 8 * width * chunk),
        name="second_pass",
    )(*args)


def pieces(value):
    rows = lax.broadcasted_iota(jnp.int32, (PAD, 256), 0)
    out = jnp.zeros((PAD, 256), f32)
    for k in range(3):
        piece = value.astype(bf16).astype(f32)
        out = jnp.where(rows == k, piece, out)
        value = value - piece
    return out.astype(bf16)


def joined(block):
    return jnp.sum(block[:, 0:1].astype(f32), axis=0, keepdims=True)


def core_sum_kernel(keep_ref, got_ref, loss_ref, other_ref, *outs, blocks):
    size = keep_ref.shape[0] // blocks
    loss = loss_ref[0:1, 0:1] + other_ref[0:1, 0:1]
    for k in range(blocks):
        at = slice(k * size, (k + 1) * size)
        outs[k][0:size, :] = (keep_ref[at, :] + got_ref[at, :].astype(f32)).astype(outs[k].dtype)
        if k:
            outs[k][size:, :] = pieces(loss)
    outs[-1][...] = jnp.broadcast_to(loss, outs[-1].shape)


def core_sum(keep, got, loss, other, blocks):
    rows, width = keep.shape
    size = rows // blocks
    return pl.pallas_call(
        functools.partial(core_sum_kernel, blocks=blocks),
        out_shape=[jax.ShapeDtypeStruct((size, width), f32)]
        + [jax.ShapeDtypeStruct((size + PAD, width), bf16)] * (blocks - 1)
        + [jax.ShapeDtypeStruct((8, 128), f32)],
        compiler_params=params(8),
        cost_estimate=cost(0, 1 << 20),
        name="core_sum",
    )(keep, got, loss, other)


def axis_sum_kernel(keep_ref, loss_ref, *refs, blocks, sources):
    got, outs = refs[:sources], refs[sources:]
    rows = keep_ref.shape[0]
    size = rows // blocks
    loss = loss_ref[0:1, 0:1]
    for ref in got:
        loss = loss + joined(ref[rows:, :])
    for k in range(blocks):
        at = slice(k * size, (k + 1) * size)
        total = keep_ref[at, :]
        for ref in got:
            total = total + ref[at, :].astype(f32)
        outs[k][0:size, :] = total.astype(outs[k].dtype)
        if k:
            outs[k][size:, :] = pieces(loss)
    outs[-1][...] = jnp.broadcast_to(loss, outs[-1].shape)


def axis_sum(keep, loss, got, blocks):
    rows, width = keep.shape
    size = rows // blocks
    return pl.pallas_call(
        functools.partial(axis_sum_kernel, blocks=blocks, sources=len(got)),
        out_shape=[jax.ShapeDtypeStruct((size, width), f32)]
        + [jax.ShapeDtypeStruct((size + PAD, width), bf16)] * (blocks - 1)
        + [jax.ShapeDtypeStruct((8, 128), f32)],
        compiler_params=params(8),
        cost_estimate=cost(0, 1 << 20),
        name="axis_sum",
    )(keep, loss, *got)


def row_kernel(keep_ref, loss_ref, raw_ref, inv_ref, *refs, sources, rows_total):
    got, (out_ref, total_ref) = refs[:sources], refs[sources:]
    rows = keep_ref.shape[0]
    loss = loss_ref[0:1, 0:1]
    grad = keep_ref[...]
    for ref in got:
        loss = loss + joined(ref[rows:, :])
        grad = grad + ref[0:rows, :].astype(f32)
    raw = raw_ref[...]
    inv = inv_ref[:, 0:1]
    out_ref[...] = inv * grad - inv * inv * inv * raw * jnp.sum(raw * grad, axis=-1, keepdims=True)
    total_ref[...] = jnp.broadcast_to(loss / rows_total, total_ref.shape)


def step_kernel(place_ref, *refs, groups):
    grads = refs[:groups]
    student_ref, teacher_ref, first_ref, second_ref = refs[groups : groups + 4]
    out_student, out_first, out_second, out_teacher = refs[-4:]
    source = pl.program_id(0)
    for k in range(groups):

        @pl.when(source == k)
        def _(k=k):
            grad = grads[k][...].astype(f32)
            first = beta_one * first_ref[...] + (1.0 - beta_one) * grad
            second = beta_two * second_ref[...] + (1.0 - beta_two) * grad * grad
            step = first / fix_one / (jnp.sqrt(second / fix_two) + 1e-08)
            student = student_ref[...]
            student = student - learn_rate * (step + decay_rate * student)
            out_student[...] = student
            out_first[...] = first
            out_second[...] = second
            out_teacher[...] = teacher_keep * teacher_ref[...] + (1.0 - teacher_keep) * student


def optimizer(place, grads, student, teacher, first, second, done, index, chunks, share):
    groups = len(grads)
    slab, total = first.shape
    chunk = share // chunks
    tile = min(chunk, 2048)
    steps = chunk // tile
    column = lambda k, j, place_ref: (place_ref[0] ^ k) * (share // tile) + index * steps + j
    sliced = pl.BlockSpec((slab, tile), lambda k, j, place_ref: (place_ref[0], column(k, j, place_ref)))
    local = pl.BlockSpec((slab, tile), lambda k, j, place_ref: (0, column(k, j, place_ref)))
    grad_specs = [
        pl.BlockSpec((slab, tile), lambda k, j, place_ref, g=g: (0, jnp.where(k == g, j, jnp.where(k < g, 0, steps - 1))))
        for g in range(groups)
    ]
    in_specs = grad_specs + [sliced, sliced, local, local]
    args = [*grads, student, teacher, first, second]
    aliases = {}
    if done is not None:
        aliases = {1 + len(args) + i: i for i in range(4)}
        in_specs += [pl.BlockSpec(memory_space=pl.ANY)] * 4
        args += list(done)
    return pl.pallas_call(
        functools.partial(step_kernel, groups=groups),
        grid_spec=pltpu.PrefetchScalarGridSpec(
            num_scalar_prefetch=1, grid=(groups, steps), in_specs=in_specs, out_specs=[local] * 4
        ),
        out_shape=[jax.ShapeDtypeStruct((slab, total), f32)] * 4,
        input_output_aliases=aliases,
        compiler_params=params(16),
        cost_estimate=cost(20 * slab * groups * chunk, 34 * slab * groups * chunk),
        name="optimizer",
    )(place, *args)


def local(
    student_patch,
    teacher_patch,
    patch_image,
    masked_rows,
    student_proto,
    teacher_proto,
    first_moment,
    second_moment,
    centre,
):
    count = masked_rows.shape[1]
    patches, width = student_patch.shape[1:]
    protos = lax.axis_size("proto")
    groups = lax.axis_size("dp")
    columns = student_proto.shape[1]
    share = columns // groups
    images = patches * protos // PATCH_IMG
    ratio = count * PATCH_IMG / patches
    rows_total = count * protos * groups
    place = lax.axis_index("dp").astype(jnp.int32).reshape(1)
    centre = centre.reshape(1, columns)

    def proto_swap(x, k):
        return lax.ppermute(x, "proto", xor_pairs(protos, k))

    def dp_swap(x, k):
        return lax.ppermute(x, "dp", xor_pairs(groups, k))

    pack, raw, inv = pick_rows(masked_rows, patch_image, student_patch[0], teacher_patch[0])
    near = [proto_swap(pack, k) for k in range(2, protos, 2)]
    ws, wt = round_protos(student_proto, teacher_proto)
    near, ws, wt = lax.optimization_barrier((near, ws, wt))
    own = jnp.concatenate([pack] + near, axis=0)
    other = proto_swap(own, 1)
    far = [dp_swap(own, k) for k in range(1, groups)]

    stats = first_pass(own, other, ws, wt, centre, count)
    stats = pl.pallas_call(
        core_join_kernel,
        out_shape=jax.ShapeDtypeStruct(stats.shape, f32),
        compiler_params=params(8),
        cost_estimate=cost(0, 1 << 20),
        name="core_join",
    )(stats, proto_swap(stats, 1))
    stats, ws, wt, *far = lax.optimization_barrier((stats, ws, wt, *far))
    far_other = [proto_swap(x, 1) for x in far]
    packs = [own, other]
    for pair in zip(far, far_other):
        packs += list(pair)
    us, ut, flipped = lay_rows(place, packs, count)

    own_ws, own_wt, own_centre = [lax.dynamic_slice_in_dim(x, place[0] * share, share, 1) for x in (ws, wt, centre)]
    stats, loss_own = pl.pallas_call(
        functools.partial(final_join_kernel, count=count, images=images, ratio=ratio),
        out_shape=[jax.ShapeDtypeStruct(stats.shape, f32), jax.ShapeDtypeStruct((8, 128), f32)],
        compiler_params=params(8),
        cost_estimate=cost(0, 1 << 20),
        name="final_join",
    )(stats, *[proto_swap(stats, k) for k in range(2, protos, 2)], own, other)
    all_stats = [stats] + [dp_swap(stats, k) for k in range(1, groups)]

    carry = None
    sent = []
    for index in range(CHUNKS):
        out = second_pass(us, ut, flipped, own_ws, own_wt, own_centre, all_stats, carry, index, CHUNKS, count)
        grads, carry = out[:groups], out[groups:]
        sent.append([grads[0]] + [dp_swap(grads[k], k) for k in range(1, groups)])
    keep, send, cross = carry
    send, sent[:-1] = lax.optimization_barrier((send, sent[:-1]))
    loss = loss_own - cross

    depth = protos // 2
    out = core_sum(keep, proto_swap(send, 1), loss, proto_swap(loss, 1), depth)
    got = [proto_swap(out[k], 2 * k) for k in range(1, depth)]
    done = None
    for index in range(CHUNKS - 1):
        done = optimizer(
            place, sent[index], student_proto, teacher_proto, first_moment, second_moment, done, index, CHUNKS, share
        )
    got, done = lax.optimization_barrier((got, done))
    out = axis_sum(out[0], out[-1], got, groups)
    got = [dp_swap(out[k], k) for k in range(1, groups)]
    done = optimizer(
        place, sent[-1], student_proto, teacher_proto, first_moment, second_moment, done, CHUNKS - 1, CHUNKS, share
    )
    row_grad, total = pl.pallas_call(
        functools.partial(row_kernel, sources=len(got), rows_total=rows_total),
        out_shape=[jax.ShapeDtypeStruct((count, width), f32), jax.ShapeDtypeStruct((8, 128), f32)],
        compiler_params=params(8),
        cost_estimate=cost(0, 1 << 20),
        name="row_grad",
    )(out[0], out[-1], raw, inv, *got)
    new_student, new_first, new_second, new_teacher = done
    return (row_grad[None], new_student, new_first, new_second, new_teacher, total[0, 0])


def solution(mesh):
    in_specs = (
        P("dp", "proto", None),
        P("dp", "proto", None),
        P("dp", "proto"),
        P("dp", "proto"),
        P(None, "proto"),
        P(None, "proto"),
        P("dp", "proto"),
        P("dp", "proto"),
        P("proto"),
    )
    out_specs = (
        P("dp", "proto", None),
        P("dp", "proto"),
        P("dp", "proto"),
        P("dp", "proto"),
        P("dp", "proto"),
        P(),
    )
    return jax.shard_map(local, mesh=mesh, in_specs=in_specs, out_specs=out_specs, check_vma=False)
```

```python
import functools

import jax
import jax.numpy as jnp
from jax import lax
from jax.experimental import pallas as pl
from jax.experimental.pallas import tpu as pltpu
from jax.sharding import PartitionSpec as P

PATCH_IMG = 256

student_temp = 0.1
teacher_temp = 0.07
beta_one = 0.9
beta_two = 0.999
fix_one = 0.9999734386011124
fix_two = 0.09520785288629038
learn_rate = 0.002
decay_rate = 0.04
teacher_keep = 0.994

log2_e = 1.4426950408889634
ln_2 = 0.6931471805599453
least = 2.0**-60
most = 2.0**120
scale_s = log2_e / student_temp
scale_t = log2_e / teacher_temp

f32 = jnp.float32
bf16 = jnp.bfloat16
PAD = 16
CHUNKS = 2


def params(mebibytes):
    return pltpu.CompilerParams(vmem_limit_bytes=mebibytes << 20)


def cost(flops, moved):
    return pl.CostEstimate(flops=flops, bytes_accessed=moved, transcendentals=0)


def in_hbm(x):
    return pltpu.with_memory_space_constraint(x, pltpu.HBM)


def xor_pairs(size, k):
    return [(i, i ^ k) for i in range(size)]


def pick_kernel(rows_ref, image_ref, student_ref, teacher_ref, pack_ref, raw_ref, inv_ref):
    patches, width = student_ref.shape
    count = rows_ref.shape[1]
    hot = lax.broadcasted_iota(jnp.int32, (patches, count), 0) == rows_ref[...]
    hot = jnp.where(hot, 1.0, 0.0).astype(bf16)

    def pick(table):
        return lax.dot_general(hot, table, (((0,), (0,)), ((), ())), preferred_element_type=f32)

    def unit(raw):
        inverse = lax.rsqrt(jnp.sum(raw * raw, axis=-1, keepdims=True) + 1e-06)
        return raw * inverse, inverse

    raw_s = pick(student_ref[...])
    unit_s, inv_s = unit(raw_s)
    unit_t, _ = unit(pick(teacher_ref[...]))
    raw_ref[...] = raw_s
    inv_ref[...] = jnp.broadcast_to(inv_s, inv_ref.shape)
    pack_ref[0:count, :] = unit_s.astype(bf16)
    pack_ref[count : 2 * count, :] = unit_t.astype(bf16)
    images = jnp.broadcast_to(image_ref[...].astype(f32), (PAD, patches)).astype(bf16)
    ids = jnp.dot(images, hot, preferred_element_type=f32)
    pack_ref[2 * count :, :] = jnp.zeros((PAD, width), bf16)
    pack_ref[2 * count :, 0:count] = ids.astype(bf16)


def pick_rows(rows, image, student, teacher):
    patches, width = student.shape
    count = rows.shape[1]
    return pl.pallas_call(
        pick_kernel,
        out_shape=[
            jax.ShapeDtypeStruct((2 * count + PAD, width), bf16),
            jax.ShapeDtypeStruct((count, width), f32),
            jax.ShapeDtypeStruct((count, 128), f32),
        ],
        compiler_params=params(2),
        cost_estimate=cost(0, 1 << 20),
        name="pick_rows",
    )(*map(in_hbm, (rows, image, student, teacher)))


def round_kernel(place_ref, s_hbm, t_hbm, ws, wt, slab_s, slab_t, buffer, sem, *, tile, depth, groups):
    width, cols = s_hbm.shape
    slab = width // groups
    steps = cols // tile
    start = pl.multiple_of(place_ref[0] * slab, slab)

    def copies(j):
        k = j % depth
        span = pl.ds(j * tile, tile)
        return [pltpu.make_async_copy(hbm.at[:, span], buffer.at[i, k], sem.at[i, k]) for i, hbm in enumerate((s_hbm, t_hbm))]

    for j in range(depth - 1):
        for copy in copies(j):
            copy.start()
    for j in range(steps):
        if j + depth - 1 < steps:
            for copy in copies(j + depth - 1):
                copy.start()
        span = slice(j * tile, (j + 1) * tile)
        for i, (copy, out, rows) in enumerate(zip(copies(j), (ws, wt), (slab_s, slab_t))):
            copy.wait()
            out[:, span] = buffer[i, j % depth].astype(bf16)
            rows[:, span] = buffer[i, j % depth, pl.ds(start, slab), :]


def round_protos(place, student, teacher, groups):
    width, cols = student.shape
    tile = min(cols, 1024)
    depth = 4
    vmem = pl.BlockSpec(memory_space=pltpu.VMEM)
    return pl.pallas_call(
        functools.partial(round_kernel, tile=tile, depth=depth, groups=groups),
        in_specs=[pl.BlockSpec(memory_space=pltpu.SMEM)] + [pl.BlockSpec(memory_space=pltpu.HBM)] * 2,
        out_specs=[vmem] * 4,
        out_shape=[jax.ShapeDtypeStruct((width, cols), bf16)] * 2
        + [jax.ShapeDtypeStruct((width // groups, cols), f32)] * 2,
        scratch_shapes=[pltpu.VMEM((2, depth, width, tile), f32), pltpu.SemaphoreType.DMA((2, depth))],
        compiler_params=params(10),
        cost_estimate=cost(0, 12 * width * cols),
        name="round_protos",
    )(place, in_hbm(student), in_hbm(teacher))


def first_kernel(own_ref, other_ref, ws_ref, wt_ref, centre_ref, out_ref, us, ut, ms, ss, mt, st, *, count):
    pack = 2 * count + PAD
    rows = us.shape[0]
    half = rows // 2
    cols = ws_ref.shape[1]
    for c, ref in enumerate((own_ref, other_ref)):
        for z in range(half // count):
            at = c * half + z * count
            us[at : at + count, :] = ref[z * pack : z * pack + count, :]
            ut[at : at + count, :] = ref[z * pack + count : z * pack + 2 * count, :]

    block = min(rows, 512)
    tile = min(cols, 1024)
    unroll = 2 if cols % (2 * tile) == 0 else 1

    def sweep(update):
        @pl.loop(0, cols // (tile * unroll))
        def _(j):
            for u in range(unroll):
                span = pl.ds(pl.multiple_of((j * unroll + u) * tile, tile), tile)
                ws = ws_ref[:, span]
                wt = wt_ref[:, span]
                shift = centre_ref[:, span] * scale_t
                for r in range(rows // block):
                    at = slice(r * block, (r + 1) * block)
                    zs = jnp.dot(us[at, :], ws, preferred_element_type=f32)
                    update([zs[:, i : i + 128] * scale_s for i in range(0, tile, 128)], ms, ss, at)
                    zt = jnp.dot(ut[at, :], wt, preferred_element_type=f32)
                    update([zt[:, i : i + 128] * scale_t - shift[:, i : i + 128] for i in range(0, tile, 128)], mt, st, at)

    def plain(parts, m_ref, s_ref, at):
        s_ref[at, :] += functools.reduce(jnp.add, [jnp.exp2(part) for part in parts])

    def running(parts, m_ref, s_ref, at):
        old = m_ref[at, :]
        new = functools.reduce(jnp.maximum, parts, old)
        total = functools.reduce(jnp.add, [jnp.exp2(part - new) for part in parts])
        s_ref[at, :] = s_ref[at, :] * jnp.exp2(old - new) + total
        m_ref[at, :] = new

    for m, s in ((ms, ss), (mt, st)):
        m[...] = jnp.zeros_like(m)
        s[...] = jnp.zeros_like(s)
    sweep(plain)
    far = jnp.zeros((rows, 1), f32)
    for s in (ss, st):
        total = jnp.sum(s[...], axis=1, keepdims=True)
        far = jnp.maximum(far, jnp.where((total > least) & (total < most), 0.0, 1.0))

    @pl.when(jnp.max(far) > 0.5)
    def _():
        for m, s in ((ms, ss), (mt, st)):
            m[...] = jnp.full_like(m, -jnp.inf)
            s[...] = jnp.zeros_like(s)
        sweep(running)

    out_ref[...] = jnp.zeros_like(out_ref)
    for k, (m, s) in enumerate(((ms, ss), (mt, st))):
        lanes = m[...]
        peak = jnp.max(lanes, axis=1, keepdims=True)
        total = jnp.sum(s[...] * jnp.exp2(lanes - peak), axis=1, keepdims=True)
        lse = jnp.broadcast_to(peak + jnp.log2(total), lanes.shape)
        out_ref[k : k + 1, :] = jnp.transpose(lse)[0:1, :]


def first_pass(own, other, ws, wt, centre, count):
    width, cols = ws.shape
    rows = 2 * own.shape[0] // (2 * count + PAD) * count
    return pl.pallas_call(
        functools.partial(first_kernel, count=count),
        in_specs=[pl.BlockSpec(memory_space=pltpu.VMEM)] * 5,
        out_shape=jax.ShapeDtypeStruct((8, rows), f32),
        scratch_shapes=[pltpu.VMEM((rows, width), bf16)] * 2 + [pltpu.VMEM((rows, 128), f32)] * 4,
        compiler_params=params((rows * (2 * width + 2048) >> 20) + 5),
        cost_estimate=cost(4 * rows * width * cols, 4 * width * cols),
        name="first_pass",
    )(own, other, ws, wt, centre)


def join(parts):
    peak = functools.reduce(jnp.maximum, parts)
    total = functools.reduce(jnp.add, [jnp.exp2(part - peak) for part in parts])
    return peak + jnp.log2(total)


def swap_blocks(x, k, size):
    n = x.shape[1] // size
    return jnp.concatenate([x[:, (j ^ k) * size : ((j ^ k) + 1) * size] for j in range(n)], axis=1)


def core_join_kernel(own_ref, other_ref, out_ref):
    half = own_ref.shape[1] // 2
    out_ref[...] = join([own_ref[...], swap_blocks(other_ref[...], 1, half)])


def final_join_kernel(*refs, count, images, ratio):
    stats, (own_ref, other_ref), (out_ref, loss_ref) = refs[:-4], refs[-4:-2], refs[-2:]
    rows = stats[0].shape[1]
    pack = 2 * count + PAD
    lse = join([swap_blocks(ref[...], k, count) for k, ref in enumerate(stats)])
    ids = jnp.concatenate(
        [
            ref[z * pack + 2 * count : (z + 1) * pack, 0:count].astype(f32)[0:8, :]
            for ref in (own_ref, other_ref)
            for z in range(rows // (2 * count))
        ],
        axis=1,
    )
    per_row = jnp.zeros_like(ids)
    for label in range(images):
        match = jnp.where(ids == label, 1.0, 0.0)
        per_row += match * jnp.sum(match, axis=1, keepdims=True)
    weight = ratio / per_row
    out_ref[...] = lse - jnp.log2(weight / student_temp)
    own = jnp.sum(weight[0:1, 0:count] * lse[0:1, 0:count] * ln_2, axis=1, keepdims=True)
    loss_ref[...] = jnp.broadcast_to(own, loss_ref.shape)


def lay_kernel(place_ref, *refs, count, groups):
    packs, (s_hbm, t_hbm), refs = refs[: 2 * groups], refs[2 * groups : 2 * groups + 2], refs[2 * groups + 2 :]
    us, ut, flipped, own_s, own_t, turned, sem = refs
    share = own_s.shape[1]
    span = pl.ds(pl.multiple_of(place_ref[0] * share, share), share)
    copies = [
        pltpu.make_async_copy(hbm.at[:, span], own, sem.at[i]) for i, (hbm, own) in enumerate(((s_hbm, own_s), (t_hbm, own_t)))
    ]
    for copy in copies:
        copy.start()
    pack = 2 * count + PAD
    at = 0
    for ref in packs:
        for z in range(ref.shape[0] // pack):
            us[at : at + count, :] = ref[z * pack : z * pack + count, :]
            ut[at : at + count, :] = ref[z * pack + count : z * pack + 2 * count, :]
            at += count
    width = us.shape[1]
    turned[...] = jnp.transpose(us[...])
    slab = width // groups
    for k in range(groups):
        start = pl.multiple_of((place_ref[0] ^ k) * slab, slab)
        flipped[k * slab : (k + 1) * slab, :] = turned[pl.ds(start, slab), :]
    for copy in copies:
        copy.wait()


def lay_rows(place, packs, ws, wt, count):
    groups = len(packs) // 2
    width, cols = ws.shape
    rows = 2 * groups * (packs[0].shape[0] // (2 * count + PAD)) * count
    vmem = pl.BlockSpec(memory_space=pltpu.VMEM)
    hbm = pl.BlockSpec(memory_space=pltpu.HBM)
    return pl.pallas_call(
        functools.partial(lay_kernel, count=count, groups=groups),
        in_specs=[pl.BlockSpec(memory_space=pltpu.SMEM)] + [vmem] * len(packs) + [hbm] * 2,
        out_shape=[jax.ShapeDtypeStruct((rows, width), bf16)] * 2
        + [jax.ShapeDtypeStruct((width, rows), bf16)]
        + [jax.ShapeDtypeStruct((width, cols // groups), bf16)] * 2,
        out_specs=[vmem] * 5,
        scratch_shapes=[pltpu.VMEM((width, rows), bf16), pltpu.SemaphoreType.DMA((2,))],
        compiler_params=params((width * rows * 2 >> 20) + 2),
        cost_estimate=cost(0, 4 << 20),
        name="lay_rows",
    )(place, *packs, in_hbm(ws), in_hbm(wt))


def pieces(value):
    rows = lax.broadcasted_iota(jnp.int32, (PAD, 256), 0)
    out = jnp.zeros((PAD, 256), f32)
    for k in range(3):
        piece = value.astype(bf16).astype(f32)
        out = jnp.where(rows == k, piece, out)
        value = value - piece
    return out.astype(bf16)


def joined(block):
    return jnp.sum(block[:, 0:1].astype(f32), axis=0, keepdims=True)


def second_kernel(us, ut, flipped, ws_ref, wt_ref, centre_ref, *refs, groups, index, chunk, last, count):
    stats, refs = refs[:groups], refs[groups:]
    seed_ref, refs = refs[0], refs[1:]
    if index:
        carry_ref, refs = refs[0], refs[1:]
    grads, refs = refs[:groups], refs[groups:]
    if last:
        keep_ref, send_ref, loss_ref, total, loss_sum, shift_s, shift_t = refs
    else:
        total, loss_ref, loss_sum, shift_s, shift_t = refs
    rows, width = us.shape
    group_rows = rows // groups
    slab = width // groups
    tile = min(chunk, 512)
    steps = chunk // tile

    total[...] = carry_ref[...] if index else jnp.zeros_like(total)
    loss_sum[...] = jnp.zeros_like(loss_sum)
    for g in range(groups):
        at = slice(g * group_rows, (g + 1) * group_rows)
        for k, shift in enumerate((shift_s, shift_t)):
            shift[at, :] = jnp.transpose(jnp.broadcast_to(stats[g][k : k + 1, :], (128, group_rows)))

    block = min(group_rows, 256)
    places = [slice(r * block, (r + 1) * block) for r in range(rows // block)]

    @pl.loop(0, steps)
    def _(j):
        span = pl.ds(pl.multiple_of(index * chunk + j * tile, tile), tile)
        ws = ws_ref[:, span]
        wt = wt_ref[:, span]
        centre = centre_ref[:, span] * scale_t

        def products(at):
            return (
                jnp.dot(us[at, :], ws, preferred_element_type=f32),
                jnp.dot(ut[at, :], wt, preferred_element_type=f32),
            )

        ready = products(places[0])
        grad = None
        for r, at in enumerate(places):
            zs, zt = ready
            if r + 1 < len(places):
                ready = products(places[r + 1])
            down_s, down_t = shift_s[at, :], shift_t[at, :]
            parts = []
            loss = None
            for i in range(0, tile, 128):
                zsi = zs[:, i : i + 128]
                ps = jnp.exp2(zsi * scale_s - down_s)
                pt = jnp.exp2(zt[:, i : i + 128] * scale_t - centre[:, i : i + 128] - down_t)
                cross = pt * zsi
                loss = cross if loss is None else loss + cross
                parts.append((ps - pt).astype(bf16))
            loss_sum[...] += jnp.sum(loss.reshape(block // 8, 8, 128), axis=0)
            logit = jnp.concatenate(parts, axis=1)
            total[at, :] += lax.dot_general(logit, ws, (((1,), (1,)), ((), ())), preferred_element_type=f32)
            part = jnp.dot(flipped[:, at], logit, preferred_element_type=f32)
            grad = part if grad is None else grad + part
        out = pl.ds(pl.multiple_of(j * tile, tile), tile)
        for k in range(groups):
            grads[k][:, out] = grad[k * slab : (k + 1) * slab, :].astype(bf16)

    done = jnp.sum(jnp.sum(loss_sum[...], axis=1, keepdims=True), axis=0, keepdims=True)
    loss = seed_ref[0:1, 0:1] - done
    loss_ref[...] = jnp.broadcast_to(loss, loss_ref.shape)
    if last:
        send_ref[rows // 2 :, :] = pieces(loss)
        depth = group_rows // (2 * count)
        for g in range(groups):
            for c, ref in enumerate((keep_ref, send_ref)):
                for z in range(depth):
                    src = g * group_rows + (c * depth + z) * count
                    dst = (z * groups + g) * count
                    ref[dst : dst + count, :] = total[src : src + count, :].astype(ref.dtype)


def second_pass(us, ut, flipped, ws, wt, centre, stats, carry, index, chunks, count):
    rows, width = us.shape
    groups = len(stats)
    slab = width // groups
    chunk = centre.shape[1] // chunks
    last = index == chunks - 1
    args = [us, ut, flipped, ws, wt, centre, *stats, *carry]
    out_shape = [jax.ShapeDtypeStruct((slab, chunk), bf16)] * groups
    scratch = [pltpu.VMEM((8, 128), f32)] + [pltpu.VMEM((rows, 128), f32)] * 2
    if last:
        out_shape += [jax.ShapeDtypeStruct((rows // 2, width), f32), jax.ShapeDtypeStruct((rows // 2 + PAD, width), bf16)]
        scratch = [pltpu.VMEM((rows, width), f32)] + scratch
    else:
        out_shape += [jax.ShapeDtypeStruct((rows, width), f32)]
    out_shape += [jax.ShapeDtypeStruct((8, 128), f32)]
    held = 2 * rows * 128 * 4 + 2 * rows * width * 4
    return pl.pallas_call(
        functools.partial(second_kernel, groups=groups, index=index, chunk=chunk, last=last, count=count),
        in_specs=[pl.BlockSpec(memory_space=pltpu.VMEM)] * len(args),
        out_shape=out_shape,
        scratch_shapes=scratch,
        compiler_params=params((held >> 20) + 4),
        cost_estimate=cost(8 * rows * width * chunk, 8 * width * chunk),
        name="second_pass",
    )(*args)


def core_sum_kernel(keep_ref, got_ref, loss_ref, *outs, blocks):
    size = keep_ref.shape[0] // blocks
    loss = loss_ref[0:1, 0:1] + joined(got_ref[keep_ref.shape[0] :, :])
    for k in range(blocks):
        at = slice(k * size, (k + 1) * size)
        outs[k][0:size, :] = (keep_ref[at, :] + got_ref[at, :].astype(f32)).astype(outs[k].dtype)
        if k:
            outs[k][size:, :] = pieces(loss)
    outs[-1][...] = jnp.broadcast_to(loss, outs[-1].shape)


def core_sum(keep, got, loss, blocks):
    rows, width = keep.shape
    size = rows // blocks
    return pl.pallas_call(
        functools.partial(core_sum_kernel, blocks=blocks),
        out_shape=[jax.ShapeDtypeStruct((size, width), f32)]
        + [jax.ShapeDtypeStruct((size + PAD, width), bf16)] * (blocks - 1)
        + [jax.ShapeDtypeStruct((8, 128), f32)],
        compiler_params=params(3),
        cost_estimate=cost(0, 1 << 20),
        name="core_sum",
    )(keep, got, loss)


def axis_sum_kernel(keep_ref, loss_ref, *refs, blocks, sources):
    got, outs = refs[:sources], refs[sources:]
    rows = keep_ref.shape[0]
    size = rows // blocks
    loss = loss_ref[0:1, 0:1]
    for ref in got:
        loss = loss + joined(ref[rows:, :])
    for k in range(blocks):
        at = slice(k * size, (k + 1) * size)
        total = keep_ref[at, :]
        for ref in got:
            total = total + ref[at, :].astype(f32)
        outs[k][0:size, :] = total.astype(outs[k].dtype)
        if k:
            outs[k][size:, :] = pieces(loss)
    outs[-1][...] = jnp.broadcast_to(loss, outs[-1].shape)


def axis_sum(keep, loss, got, blocks):
    rows, width = keep.shape
    size = rows // blocks
    return pl.pallas_call(
        functools.partial(axis_sum_kernel, blocks=blocks, sources=len(got)),
        out_shape=[jax.ShapeDtypeStruct((size, width), f32)]
        + [jax.ShapeDtypeStruct((size + PAD, width), bf16)] * (blocks - 1)
        + [jax.ShapeDtypeStruct((8, 128), f32)],
        compiler_params=params(3),
        cost_estimate=cost(0, 1 << 20),
        name="axis_sum",
    )(keep, loss, *got)


def row_kernel(keep_ref, loss_ref, raw_ref, inv_ref, *refs, sources, rows_total):
    got, (out_ref, total_ref) = refs[:sources], refs[sources:]
    rows = keep_ref.shape[0]
    loss = loss_ref[0:1, 0:1]
    grad = keep_ref[...]
    for ref in got:
        loss = loss + joined(ref[rows:, :])
        grad = grad + ref[0:rows, :].astype(f32)
    raw = raw_ref[...]
    inv = inv_ref[:, 0:1]
    out_ref[...] = inv * grad - inv * inv * inv * raw * jnp.sum(raw * grad, axis=-1, keepdims=True)
    total_ref[0, 0] = jnp.sum(loss) / rows_total


def step_kernel(place_ref, *refs, groups, index, chunk, share):
    grads = refs[:groups]
    student_ref, teacher_ref, first_ref, second_ref = refs[groups : groups + 4]
    outs, stage, sem = refs[-6:-2], refs[-2], refs[-1]
    copies = []
    for k in range(groups):
        span = pl.ds(pl.multiple_of((place_ref[0] ^ k) * share + index * chunk, chunk), chunk)
        grad = grads[k][...].astype(f32)
        first = beta_one * first_ref[:, span] + (1.0 - beta_one) * grad
        second = beta_two * second_ref[:, span] + (1.0 - beta_two) * grad * grad
        step = first / fix_one / (jnp.sqrt(second / fix_two) + 1e-08)
        student = student_ref[:, span]
        student = student - learn_rate * (step + decay_rate * student)
        teacher = teacher_keep * teacher_ref[:, span] + (1.0 - teacher_keep) * student
        for i, value in enumerate((student, first, second, teacher)):
            stage[k, i] = value
            copies.append(pltpu.make_async_copy(stage.at[k, i], outs[i].at[:, span], sem.at[k, i]))
            copies[-1].start()
    for copy in copies:
        copy.wait()


def optimizer(place, grads, student, teacher, first, second, done, index, chunks, share):
    groups = len(grads)
    slab, total = first.shape
    chunk = share // chunks
    vmem = pl.BlockSpec(memory_space=pltpu.VMEM)
    hbm = pl.BlockSpec(memory_space=pltpu.HBM)
    in_specs = [pl.BlockSpec(memory_space=pltpu.SMEM)] + [vmem] * (groups + 4)
    args = [place, *grads, student, teacher, first, second]
    aliases = {}
    if done is not None:
        aliases = {len(args) + i: i for i in range(4)}
        in_specs += [hbm] * 4
        args += list(done)
    return pl.pallas_call(
        functools.partial(step_kernel, groups=groups, index=index, chunk=chunk, share=share),
        in_specs=in_specs,
        out_specs=[hbm] * 4,
        out_shape=[jax.ShapeDtypeStruct((slab, total), f32)] * 4,
        scratch_shapes=[pltpu.VMEM((groups, 4, slab, chunk), f32), pltpu.SemaphoreType.DMA((groups, 4))],
        input_output_aliases=aliases,
        compiler_params=params(11),
        cost_estimate=cost(20 * slab * groups * chunk, 16 * slab * groups * chunk),
        name="optimizer",
    )(*args)


def local(
    student_patch,
    teacher_patch,
    patch_image,
    masked_rows,
    student_proto,
    teacher_proto,
    first_moment,
    second_moment,
    centre,
):
    count = masked_rows.shape[1]
    patches, width = student_patch.shape[1:]
    protos = lax.axis_size("proto")
    groups = lax.axis_size("dp")
    columns = student_proto.shape[1]
    share = columns // groups
    images = patches * protos // PATCH_IMG
    ratio = count * PATCH_IMG / patches
    rows_total = count * protos * groups
    place = lax.axis_index("dp").astype(jnp.int32).reshape(1)
    centre = centre.reshape(1, columns)

    def proto_swap(x, k):
        return lax.ppermute(x, "proto", xor_pairs(protos, k))

    def dp_swap(x, k):
        return lax.ppermute(x, "dp", xor_pairs(groups, k))

    pack, raw, inv = pick_rows(masked_rows, patch_image, student_patch[0], teacher_patch[0])
    near = [proto_swap(pack, k) for k in range(2, protos, 2)]
    ws, wt, slab_s, slab_t = round_protos(place, student_proto, teacher_proto, groups)
    near, ws, wt = lax.optimization_barrier((near, ws, wt))
    own = jnp.concatenate([pack] + near, axis=0)
    other = proto_swap(own, 1)
    far = [dp_swap(own, k) for k in range(1, groups)]

    stats = first_pass(own, other, ws, wt, centre, count)
    stats = pl.pallas_call(
        core_join_kernel,
        out_shape=jax.ShapeDtypeStruct(stats.shape, f32),
        compiler_params=params(3),
        cost_estimate=cost(0, 1 << 20),
        name="core_join",
    )(stats, proto_swap(stats, 1))
    stats, *far = lax.optimization_barrier((stats, *far))
    far_other = [proto_swap(x, 1) for x in far]
    packs = [own, other]
    for pair in zip(far, far_other):
        packs += list(pair)
    us, ut, flipped, own_ws, own_wt = lay_rows(place, packs, ws, wt, count)

    own_centre = lax.dynamic_slice_in_dim(centre, place[0] * share, share, 1)
    near = [proto_swap(stats, k) for k in range(2, protos, 2)]
    stats, loss_own = pl.pallas_call(
        functools.partial(final_join_kernel, count=count, images=images, ratio=ratio),
        out_shape=[jax.ShapeDtypeStruct(stats.shape, f32), jax.ShapeDtypeStruct((8, 128), f32)],
        compiler_params=params(3),
        cost_estimate=cost(0, 1 << 20),
        name="final_join",
    )(stats, *near, own, other)
    all_stats = [stats] + [dp_swap(stats, k) for k in range(1, groups)]

    carry = [loss_own]
    sent = []
    for index in range(CHUNKS):
        out = second_pass(us, ut, flipped, own_ws, own_wt, own_centre, all_stats, carry, index, CHUNKS, count)
        grads, carry = out[:groups], out[: groups - 1 : -1]
        if index + 1 < CHUNKS:
            sent.append([grads[0]] + [dp_swap(grads[k], k) for k in range(1, groups)])
    loss, send, keep = carry
    send, sent = lax.optimization_barrier((send, sent))
    depth = protos // 2
    out = core_sum(keep, proto_swap(send, 1), loss, depth)
    got = [proto_swap(out[k], 2 * k) for k in range(1, depth)]
    sent.append([grads[0]] + [dp_swap(grads[k], k) for k in range(1, groups)])
    done = None
    for index in range(CHUNKS - 1):
        done = optimizer(
            place, sent[index], slab_s, slab_t, first_moment, second_moment, done, index, CHUNKS, share
        )
    got, done = lax.optimization_barrier((got, done))
    out = axis_sum(out[0], out[-1], got, groups)
    got = [dp_swap(out[k], k) for k in range(1, groups)]
    done = optimizer(
        place, sent[-1], slab_s, slab_t, first_moment, second_moment, done, CHUNKS - 1, CHUNKS, share
    )
    got, done = lax.optimization_barrier((got, done))
    row_grad, total = pl.pallas_call(
        functools.partial(row_kernel, sources=len(got), rows_total=rows_total),
        out_shape=[jax.ShapeDtypeStruct((count, width), f32), jax.ShapeDtypeStruct((1, 1), f32)],
        out_specs=[pl.BlockSpec(memory_space=pltpu.VMEM), pl.BlockSpec(memory_space=pltpu.SMEM)],
        compiler_params=params(3),
        cost_estimate=cost(0, 1 << 20),
        name="row_grad",
    )(out[0], out[-1], raw, inv, *got)
    new_student, new_first, new_second, new_teacher = done
    return (row_grad[None], new_student, new_first, new_second, new_teacher, total.reshape(()))


def solution(mesh):
    in_specs = (
        P("dp", "proto", None),
        P("dp", "proto", None),
        P("dp", "proto"),
        P("dp", "proto"),
        P(None, "proto"),
        P(None, "proto"),
        P("dp", "proto"),
        P("dp", "proto"),
        P("proto"),
    )
    out_specs = (
        P("dp", "proto", None),
        P("dp", "proto"),
        P("dp", "proto"),
        P("dp", "proto"),
        P("dp", "proto"),
        P(),
    )
    return jax.shard_map(local, mesh=mesh, in_specs=in_specs, out_specs=out_specs, check_vma=False)
```

```python
import functools

import jax
import jax.numpy as jnp
from jax import lax
from jax.experimental import pallas as pl
from jax.experimental.pallas import tpu as pltpu
from jax.sharding import PartitionSpec as P

PATCH_IMG = 256

student_temp = 0.1
teacher_temp = 0.07
beta_one = 0.9
beta_two = 0.999
fix_one = 0.9999734386011124
fix_two = 0.09520785288629038
learn_rate = 0.002
decay_rate = 0.04
teacher_keep = 0.994

log2_e = 1.4426950408889634
ln_2 = 0.6931471805599453
least = 2.0**-60
most = 2.0**120
scale_s = log2_e / student_temp
scale_t = log2_e / teacher_temp

f32 = jnp.float32
bf16 = jnp.bfloat16
PAD = 16
CHUNKS = 2


def params(mebibytes):
    return pltpu.CompilerParams(vmem_limit_bytes=mebibytes << 20)


def cost(flops, moved):
    return pl.CostEstimate(flops=flops, bytes_accessed=moved, transcendentals=0)


def in_hbm(x):
    return pltpu.with_memory_space_constraint(x, pltpu.HBM)


def xor_pairs(size, k):
    return [(i, i ^ k) for i in range(size)]


def pick_kernel(rows_ref, image_ref, student_ref, teacher_ref, pack_ref, raw_ref, inv_ref):
    patches, width = student_ref.shape
    count = rows_ref.shape[1]
    hot = lax.broadcasted_iota(jnp.int32, (patches, count), 0) == rows_ref[...]
    hot = jnp.where(hot, 1.0, 0.0).astype(bf16)

    def pick(table):
        return lax.dot_general(hot, table, (((0,), (0,)), ((), ())), preferred_element_type=f32)

    def unit(raw):
        inverse = lax.rsqrt(jnp.sum(raw * raw, axis=-1, keepdims=True) + 1e-06)
        return raw * inverse, inverse

    raw_s = pick(student_ref[...])
    unit_s, inv_s = unit(raw_s)
    unit_t, _ = unit(pick(teacher_ref[...]))
    raw_ref[...] = raw_s
    inv_ref[...] = jnp.broadcast_to(inv_s, inv_ref.shape)
    pack_ref[0:count, :] = unit_s.astype(bf16)
    pack_ref[count : 2 * count, :] = unit_t.astype(bf16)
    images = jnp.broadcast_to(image_ref[...].astype(f32), (PAD, patches)).astype(bf16)
    ids = jnp.dot(images, hot, preferred_element_type=f32)
    pack_ref[2 * count :, :] = jnp.zeros((PAD, width), bf16)
    pack_ref[2 * count :, 0:count] = ids.astype(bf16)


def pick_rows(rows, image, student, teacher):
    patches, width = student.shape
    count = rows.shape[1]
    return pl.pallas_call(
        pick_kernel,
        out_shape=[
            jax.ShapeDtypeStruct((2 * count + PAD, width), bf16),
            jax.ShapeDtypeStruct((count, width), f32),
            jax.ShapeDtypeStruct((count, 128), f32),
        ],
        compiler_params=params(2),
        cost_estimate=cost(0, 1 << 20),
        name="pick_rows",
    )(*map(in_hbm, (rows, image, student, teacher)))


def round_kernel(s_hbm, t_hbm, ws, wt, buffer, sem, *, tile, depth):
    steps = ws.shape[1] // tile

    def copies(j):
        k = j % depth
        span = pl.ds(j * tile, tile)
        return [pltpu.make_async_copy(hbm.at[:, span], buffer.at[i, k], sem.at[i, k]) for i, hbm in enumerate((s_hbm, t_hbm))]

    for j in range(min(depth - 1, steps)):
        for copy in copies(j):
            copy.start()
    for j in range(steps):
        if j + depth - 1 < steps:
            for copy in copies(j + depth - 1):
                copy.start()
        for i, (copy, out) in enumerate(zip(copies(j), (ws, wt))):
            copy.wait()
            out[:, j * tile : (j + 1) * tile] = buffer[i, j % depth].astype(bf16)


def round_protos(student, teacher):
    width, cols = student.shape
    half = cols // 2
    tile = min(half, 1024)
    depth = 4
    return pl.pallas_call(
        functools.partial(round_kernel, tile=tile, depth=depth),
        in_specs=[pl.BlockSpec(memory_space=pltpu.HBM)] * 2,
        out_specs=[pl.BlockSpec(memory_space=pltpu.VMEM)] * 2,
        out_shape=[jax.ShapeDtypeStruct((width, half), bf16)] * 2,
        scratch_shapes=[pltpu.VMEM((2, depth, width, tile), f32), pltpu.SemaphoreType.DMA((2, depth))],
        compiler_params=params(10),
        cost_estimate=cost(0, 12 * width * half),
        name="round_protos",
    )(in_hbm(student), in_hbm(teacher))


def first_kernel(
    own_ref, other_ref, ws_ref, wt_ref, centre_ref, s_hbm, t_hbm, out_ref, us, ut, ms, ss, mt, st, rest, sem, *, count
):
    pack = 2 * count + PAD
    rows = us.shape[0]
    half = rows // 2
    cols = ws_ref.shape[1]
    tile = min(cols, 1024)
    unroll = 2 if cols % (2 * tile) == 0 else 1
    copies = []
    for j in range(cols // tile):
        for i, hbm in enumerate((s_hbm, t_hbm)):
            span = slice(j * tile, (j + 1) * tile)
            copies.append(pltpu.make_async_copy(hbm.at[:, pl.ds(cols + j * tile, tile)], rest.at[i, :, span], sem.at[i, j]))
            copies[-1].start()
    for c, ref in enumerate((own_ref, other_ref)):
        for z in range(half // count):
            at = c * half + z * count
            us[at : at + count, :] = ref[z * pack : z * pack + count, :]
            ut[at : at + count, :] = ref[z * pack + count : z * pack + 2 * count, :]

    block = min(rows, 512)

    def sweep(update, second):
        @pl.loop(0, cols // (tile * unroll))
        def _(j):
            for u in range(unroll):
                span = pl.ds(pl.multiple_of((j * unroll + u) * tile, tile), tile)
                if second:
                    ws = rest[0, :, span].astype(bf16)
                    wt = rest[1, :, span].astype(bf16)
                    place = pl.ds(pl.multiple_of(cols + (j * unroll + u) * tile, tile), tile)
                else:
                    ws = ws_ref[:, span]
                    wt = wt_ref[:, span]
                    place = span
                shift = centre_ref[:, place] * scale_t
                for r in range(rows // block):
                    at = slice(r * block, (r + 1) * block)
                    zs = jnp.dot(us[at, :], ws, preferred_element_type=f32)
                    update([zs[:, i : i + 128] * scale_s for i in range(0, tile, 128)], ms, ss, at)
                    zt = jnp.dot(ut[at, :], wt, preferred_element_type=f32)
                    update([zt[:, i : i + 128] * scale_t - shift[:, i : i + 128] for i in range(0, tile, 128)], mt, st, at)

    def plain(parts, m_ref, s_ref, at):
        s_ref[at, :] += functools.reduce(jnp.add, [jnp.exp2(part) for part in parts])

    def running(parts, m_ref, s_ref, at):
        old = m_ref[at, :]
        new = functools.reduce(jnp.maximum, parts, old)
        total = functools.reduce(jnp.add, [jnp.exp2(part - new) for part in parts])
        s_ref[at, :] = s_ref[at, :] * jnp.exp2(old - new) + total
        m_ref[at, :] = new

    for m, s in ((ms, ss), (mt, st)):
        m[...] = jnp.zeros_like(m)
        s[...] = jnp.zeros_like(s)
    sweep(plain, False)
    for copy in copies:
        copy.wait()
    sweep(plain, True)
    far = jnp.zeros((rows, 1), f32)
    for s in (ss, st):
        total = jnp.sum(s[...], axis=1, keepdims=True)
        far = jnp.maximum(far, jnp.where((total > least) & (total < most), 0.0, 1.0))

    @pl.when(jnp.max(far) > 0.5)
    def _():
        for m, s in ((ms, ss), (mt, st)):
            m[...] = jnp.full_like(m, -jnp.inf)
            s[...] = jnp.zeros_like(s)
        sweep(running, False)
        sweep(running, True)

    out_ref[...] = jnp.zeros_like(out_ref)
    for k, (m, s) in enumerate(((ms, ss), (mt, st))):
        lanes = m[...]
        peak = jnp.max(lanes, axis=1, keepdims=True)
        total = jnp.sum(s[...] * jnp.exp2(lanes - peak), axis=1, keepdims=True)
        lse = jnp.broadcast_to(peak + jnp.log2(total), lanes.shape)
        out_ref[k : k + 1, :] = jnp.transpose(lse)[0:1, :]


def first_pass(own, other, ws, wt, centre, student, teacher, count):
    width, cols = ws.shape
    tile = min(cols, 1024)
    rows = 2 * own.shape[0] // (2 * count + PAD) * count
    return pl.pallas_call(
        functools.partial(first_kernel, count=count),
        in_specs=[pl.BlockSpec(memory_space=pltpu.VMEM)] * 5 + [pl.BlockSpec(memory_space=pltpu.HBM)] * 2,
        out_shape=jax.ShapeDtypeStruct((8, rows), f32),
        scratch_shapes=[pltpu.VMEM((rows, width), bf16)] * 2
        + [pltpu.VMEM((rows, 128), f32)] * 4
        + [pltpu.VMEM((2, width, cols), f32), pltpu.SemaphoreType.DMA((2, cols // tile))],
        compiler_params=params((rows * (2 * width + 2048) + 8 * width * cols >> 20) + 7),
        cost_estimate=cost(8 * rows * width * cols, 12 * width * cols),
        name="first_pass",
    )(own, other, ws, wt, centre, in_hbm(student), in_hbm(teacher))


def join(parts):
    peak = functools.reduce(jnp.maximum, parts)
    total = functools.reduce(jnp.add, [jnp.exp2(part - peak) for part in parts])
    return peak + jnp.log2(total)


def swap_blocks(x, k, size):
    n = x.shape[1] // size
    return jnp.concatenate([x[:, (j ^ k) * size : ((j ^ k) + 1) * size] for j in range(n)], axis=1)


def core_join_kernel(own_ref, other_ref, out_ref):
    half = own_ref.shape[1] // 2
    out_ref[...] = join([own_ref[...], swap_blocks(other_ref[...], 1, half)])


def final_join_kernel(*refs, count, images, ratio):
    stats, (own_ref, other_ref), (out_ref, loss_ref) = refs[:-4], refs[-4:-2], refs[-2:]
    rows = stats[0].shape[1]
    pack = 2 * count + PAD
    lse = join([swap_blocks(ref[...], k, count) for k, ref in enumerate(stats)])
    ids = jnp.concatenate(
        [
            ref[z * pack + 2 * count : (z + 1) * pack, 0:count].astype(f32)[0:8, :]
            for ref in (own_ref, other_ref)
            for z in range(rows // (2 * count))
        ],
        axis=1,
    )
    per_row = jnp.zeros_like(ids)
    for label in range(images):
        match = jnp.where(ids == label, 1.0, 0.0)
        per_row += match * jnp.sum(match, axis=1, keepdims=True)
    weight = ratio / per_row
    out_ref[...] = lse - jnp.log2(weight / student_temp)
    own = jnp.sum(weight[0:1, 0:count] * lse[0:1, 0:count] * ln_2, axis=1, keepdims=True)
    loss_ref[...] = jnp.broadcast_to(own, loss_ref.shape)


def lay_kernel(place_ref, *refs, count, groups):
    packs, (s_hbm, t_hbm), refs = refs[: 2 * groups], refs[2 * groups : 2 * groups + 2], refs[2 * groups + 2 :]
    us, ut, flipped, own_s, own_t, turned, buffer, sem = refs
    share = own_s.shape[1]
    tile = share // sem.shape[1]
    copies = []
    for j in range(share // tile):
        span = pl.ds(pl.multiple_of(place_ref[0] * share + j * tile, tile), tile)
        inner = slice(j * tile, (j + 1) * tile)
        for i, (hbm, own) in enumerate(((s_hbm, own_s), (t_hbm, own_t))):
            copy = pltpu.make_async_copy(hbm.at[:, span], buffer.at[i, :, inner], sem.at[i, j])
            copy.start()
            copies.append((copy, i, own, inner))
    pack = 2 * count + PAD
    at = 0
    for ref in packs:
        for z in range(ref.shape[0] // pack):
            us[at : at + count, :] = ref[z * pack : z * pack + count, :]
            ut[at : at + count, :] = ref[z * pack + count : z * pack + 2 * count, :]
            at += count
    width = us.shape[1]
    turned[...] = jnp.transpose(us[...])
    slab = width // groups
    for k in range(groups):
        start = pl.multiple_of((place_ref[0] ^ k) * slab, slab)
        flipped[k * slab : (k + 1) * slab, :] = turned[pl.ds(start, slab), :]
    for copy, i, own, inner in copies:
        copy.wait()
        own[:, inner] = buffer[i, :, inner].astype(bf16)


def lay_rows(place, packs, student, teacher, count):
    groups = len(packs) // 2
    width, cols = student.shape
    share = cols // groups
    tile = min(share, 1024)
    rows = 2 * groups * (packs[0].shape[0] // (2 * count + PAD)) * count
    vmem = pl.BlockSpec(memory_space=pltpu.VMEM)
    hbm = pl.BlockSpec(memory_space=pltpu.HBM)
    return pl.pallas_call(
        functools.partial(lay_kernel, count=count, groups=groups),
        in_specs=[pl.BlockSpec(memory_space=pltpu.SMEM)] + [vmem] * len(packs) + [hbm] * 2,
        out_shape=[jax.ShapeDtypeStruct((rows, width), bf16)] * 2
        + [jax.ShapeDtypeStruct((width, rows), bf16)]
        + [jax.ShapeDtypeStruct((width, share), bf16)] * 2,
        out_specs=[vmem] * 5,
        scratch_shapes=[
            pltpu.VMEM((width, rows), bf16),
            pltpu.VMEM((2, width, share), f32),
            pltpu.SemaphoreType.DMA((2, share // tile)),
        ],
        compiler_params=params((width * rows * 2 + 8 * width * share >> 20) + 2),
        cost_estimate=cost(0, 4 << 20),
        name="lay_rows",
    )(place, *packs, in_hbm(student), in_hbm(teacher))


def pieces(value):
    rows = lax.broadcasted_iota(jnp.int32, (PAD, 256), 0)
    out = jnp.zeros((PAD, 256), f32)
    for k in range(3):
        piece = value.astype(bf16).astype(f32)
        out = jnp.where(rows == k, piece, out)
        value = value - piece
    return out.astype(bf16)


def joined(block):
    return jnp.sum(block[:, 0:1].astype(f32), axis=0, keepdims=True)


def second_kernel(us, ut, flipped, ws_ref, wt_ref, centre_ref, *refs, groups, index, chunk, last, count):
    stats, refs = refs[:groups], refs[groups:]
    seed_ref, refs = refs[0], refs[1:]
    if index:
        carry_ref, refs = refs[0], refs[1:]
    else:
        (place_ref, *protos), refs = refs[:3], refs[3:]
        sem, refs = refs[-1], refs[:-1]
    grads, refs = refs[:groups], refs[groups:]
    if last:
        keep_ref, send_ref, loss_ref, total, loss_sum, shift_s, shift_t = refs
    else:
        total, loss_ref, *slabs, loss_sum, shift_s, shift_t = refs
    rows, width = us.shape
    group_rows = rows // groups
    slab = width // groups
    copies = []
    if not index:
        start = pl.multiple_of(place_ref[0] * slab, slab)
        for i, (hbm, out) in enumerate(zip(protos, slabs)):
            copies.append(pltpu.make_async_copy(hbm.at[pl.ds(start, slab), :], out, sem.at[i]))
            copies[-1].start()
    tile = min(chunk, 512)
    steps = chunk // tile

    total[...] = carry_ref[...] if index else jnp.zeros_like(total)
    loss_sum[...] = jnp.zeros_like(loss_sum)
    for g in range(groups):
        at = slice(g * group_rows, (g + 1) * group_rows)
        for k, shift in enumerate((shift_s, shift_t)):
            shift[at, :] = jnp.transpose(jnp.broadcast_to(stats[g][k : k + 1, :], (128, group_rows)))

    block = min(group_rows, 256)
    places = [slice(r * block, (r + 1) * block) for r in range(rows // block)]

    @pl.loop(0, steps)
    def _(j):
        span = pl.ds(pl.multiple_of(index * chunk + j * tile, tile), tile)
        ws = ws_ref[:, span]
        wt = wt_ref[:, span]
        centre = centre_ref[:, span] * scale_t

        def products(at):
            return (
                jnp.dot(us[at, :], ws, preferred_element_type=f32),
                jnp.dot(ut[at, :], wt, preferred_element_type=f32),
            )

        ready = products(places[0])
        grad = None
        for r, at in enumerate(places):
            zs, zt = ready
            if r + 1 < len(places):
                ready = products(places[r + 1])
            down_s, down_t = shift_s[at, :], shift_t[at, :]
            parts = []
            loss = None
            for i in range(0, tile, 128):
                zsi = zs[:, i : i + 128]
                ps = jnp.exp2(zsi * scale_s - down_s)
                pt = jnp.exp2(zt[:, i : i + 128] * scale_t - centre[:, i : i + 128] - down_t)
                cross = pt * zsi
                loss = cross if loss is None else loss + cross
                parts.append((ps - pt).astype(bf16))
            loss_sum[...] += jnp.sum(loss.reshape(block // 8, 8, 128), axis=0)
            logit = jnp.concatenate(parts, axis=1)
            total[at, :] += lax.dot_general(logit, ws, (((1,), (1,)), ((), ())), preferred_element_type=f32)
            part = jnp.dot(flipped[:, at], logit, preferred_element_type=f32)
            grad = part if grad is None else grad + part
        out = pl.ds(pl.multiple_of(j * tile, tile), tile)
        for k in range(groups):
            grads[k][:, out] = grad[k * slab : (k + 1) * slab, :].astype(bf16)

    done = jnp.sum(jnp.sum(loss_sum[...], axis=1, keepdims=True), axis=0, keepdims=True)
    loss = seed_ref[0:1, 0:1] - done
    loss_ref[...] = jnp.broadcast_to(loss, loss_ref.shape)
    for copy in copies:
        copy.wait()
    if last:
        send_ref[rows // 2 :, :] = pieces(loss)
        depth = group_rows // (2 * count)
        for g in range(groups):
            for c, ref in enumerate((keep_ref, send_ref)):
                for z in range(depth):
                    src = g * group_rows + (c * depth + z) * count
                    dst = (z * groups + g) * count
                    ref[dst : dst + count, :] = total[src : src + count, :].astype(ref.dtype)


def second_pass(place, us, ut, flipped, ws, wt, centre, stats, carry, student, teacher, index, chunks, count):
    rows, width = us.shape
    groups = len(stats)
    slab = width // groups
    chunk = centre.shape[1] // chunks
    last = index == chunks - 1
    args = [us, ut, flipped, ws, wt, centre, *stats, *carry]
    in_specs = [pl.BlockSpec(memory_space=pltpu.VMEM)] * len(args)
    out_shape = [jax.ShapeDtypeStruct((slab, chunk), bf16)] * groups
    scratch = [pltpu.VMEM((8, 128), f32)] + [pltpu.VMEM((rows, 128), f32)] * 2
    if last:
        out_shape += [jax.ShapeDtypeStruct((rows // 2, width), f32), jax.ShapeDtypeStruct((rows // 2 + PAD, width), bf16)]
        scratch = [pltpu.VMEM((rows, width), f32)] + scratch
    else:
        out_shape += [jax.ShapeDtypeStruct((rows, width), f32)]
    out_shape += [jax.ShapeDtypeStruct((8, 128), f32)]
    if not index:
        args += [place, in_hbm(student), in_hbm(teacher)]
        in_specs += [pl.BlockSpec(memory_space=pltpu.SMEM)] + [pl.BlockSpec(memory_space=pltpu.HBM)] * 2
        out_shape += [jax.ShapeDtypeStruct((slab, student.shape[1]), f32)] * 2
        scratch += [pltpu.SemaphoreType.DMA((2,))]
    held = 2 * rows * 128 * 4 + 2 * rows * width * 4
    return pl.pallas_call(
        functools.partial(second_kernel, groups=groups, index=index, chunk=chunk, last=last, count=count),
        in_specs=in_specs,
        out_specs=[pl.BlockSpec(memory_space=pltpu.VMEM)] * len(out_shape),
        out_shape=out_shape,
        scratch_shapes=scratch,
        compiler_params=params((held >> 20) + 4),
        cost_estimate=cost(8 * rows * width * chunk, 8 * width * chunk),
        name="second_pass",
    )(*args)


def core_sum_kernel(keep_ref, got_ref, loss_ref, *outs, blocks):
    size = keep_ref.shape[0] // blocks
    loss = loss_ref[0:1, 0:1] + joined(got_ref[keep_ref.shape[0] :, :])
    for k in range(blocks):
        at = slice(k * size, (k + 1) * size)
        outs[k][0:size, :] = (keep_ref[at, :] + got_ref[at, :].astype(f32)).astype(outs[k].dtype)
        if k:
            outs[k][size:, :] = pieces(loss)
    outs[-1][...] = jnp.broadcast_to(loss, outs[-1].shape)


def core_sum(keep, got, loss, blocks):
    rows, width = keep.shape
    size = rows // blocks
    return pl.pallas_call(
        functools.partial(core_sum_kernel, blocks=blocks),
        out_shape=[jax.ShapeDtypeStruct((size, width), f32)]
        + [jax.ShapeDtypeStruct((size + PAD, width), bf16)] * (blocks - 1)
        + [jax.ShapeDtypeStruct((8, 128), f32)],
        compiler_params=params(3),
        cost_estimate=cost(0, 1 << 20),
        name="core_sum",
    )(keep, got, loss)


def axis_sum_kernel(keep_ref, loss_ref, *refs, blocks, sources):
    got, outs = refs[:sources], refs[sources:]
    rows = keep_ref.shape[0]
    size = rows // blocks
    loss = loss_ref[0:1, 0:1]
    for ref in got:
        loss = loss + joined(ref[rows:, :])
    for k in range(blocks):
        at = slice(k * size, (k + 1) * size)
        total = keep_ref[at, :]
        for ref in got:
            total = total + ref[at, :].astype(f32)
        outs[k][0:size, :] = total.astype(outs[k].dtype)
        if k:
            outs[k][size:, :] = pieces(loss)
    outs[-1][...] = jnp.broadcast_to(loss, outs[-1].shape)


def axis_sum(keep, loss, got, blocks):
    rows, width = keep.shape
    size = rows // blocks
    return pl.pallas_call(
        functools.partial(axis_sum_kernel, blocks=blocks, sources=len(got)),
        out_shape=[jax.ShapeDtypeStruct((size, width), f32)]
        + [jax.ShapeDtypeStruct((size + PAD, width), bf16)] * (blocks - 1)
        + [jax.ShapeDtypeStruct((8, 128), f32)],
        compiler_params=params(3),
        cost_estimate=cost(0, 1 << 20),
        name="axis_sum",
    )(keep, loss, *got)


def row_kernel(keep_ref, loss_ref, raw_ref, inv_ref, *refs, sources, rows_total):
    got, (out_ref, total_ref) = refs[:sources], refs[sources:]
    rows = keep_ref.shape[0]
    loss = loss_ref[0:1, 0:1]
    grad = keep_ref[...]
    for ref in got:
        loss = loss + joined(ref[rows:, :])
        grad = grad + ref[0:rows, :].astype(f32)
    raw = raw_ref[...]
    inv = inv_ref[:, 0:1]
    out_ref[...] = inv * grad - inv * inv * inv * raw * jnp.sum(raw * grad, axis=-1, keepdims=True)
    total_ref[0, 0] = jnp.sum(loss) / rows_total


def step_kernel(place_ref, *refs, jobs, chunk, share):
    grads = refs[: len(jobs)]
    student_ref, teacher_ref, first_ref, second_ref = refs[len(jobs) : len(jobs) + 4]
    outs, stage, sem = refs[-6:-2], refs[-2], refs[-1]
    copies = []
    for k, (source, index) in enumerate(jobs):
        span = pl.ds(pl.multiple_of((place_ref[0] ^ source) * share + index * chunk, chunk), chunk)
        grad = grads[k][...].astype(f32)
        first = beta_one * first_ref[:, span] + (1.0 - beta_one) * grad
        second = beta_two * second_ref[:, span] + (1.0 - beta_two) * grad * grad
        step = first / fix_one / (jnp.sqrt(second / fix_two) + 1e-08)
        student = student_ref[:, span]
        student = student - learn_rate * (step + decay_rate * student)
        teacher = teacher_keep * teacher_ref[:, span] + (1.0 - teacher_keep) * student
        for i, value in enumerate((student, first, second, teacher)):
            stage[k, i] = value
            copies.append(pltpu.make_async_copy(stage.at[k, i], outs[i].at[:, span], sem.at[k, i]))
            copies[-1].start()
    for copy in copies:
        copy.wait()


def optimizer(place, jobs, student, teacher, first, second, done, share):
    jobs, grads = list(jobs), list(jobs.values())
    slab, total = first.shape
    chunk = grads[0].shape[1]
    vmem = pl.BlockSpec(memory_space=pltpu.VMEM)
    hbm = pl.BlockSpec(memory_space=pltpu.HBM)
    in_specs = [pl.BlockSpec(memory_space=pltpu.SMEM)] + [vmem] * (len(jobs) + 4)
    args = [place, *grads, student, teacher, first, second]
    aliases = {}
    if done is not None:
        aliases = {len(args) + i: i for i in range(4)}
        in_specs += [hbm] * 4
        args += list(done)
    return pl.pallas_call(
        functools.partial(step_kernel, jobs=jobs, chunk=chunk, share=share),
        in_specs=in_specs,
        out_specs=[hbm] * 4,
        out_shape=[jax.ShapeDtypeStruct((slab, total), f32)] * 4,
        scratch_shapes=[pltpu.VMEM((len(jobs), 4, slab, chunk), f32), pltpu.SemaphoreType.DMA((len(jobs), 4))],
        input_output_aliases=aliases,
        compiler_params=params((len(jobs) * 16 * slab * chunk >> 20) + 3),
        cost_estimate=cost(20 * slab * len(jobs) * chunk, 16 * slab * len(jobs) * chunk),
        name="optimizer",
    )(*args)


def local(
    student_patch,
    teacher_patch,
    patch_image,
    masked_rows,
    student_proto,
    teacher_proto,
    first_moment,
    second_moment,
    centre,
):
    count = masked_rows.shape[1]
    patches, width = student_patch.shape[1:]
    protos = lax.axis_size("proto")
    groups = lax.axis_size("dp")
    columns = student_proto.shape[1]
    share = columns // groups
    images = patches * protos // PATCH_IMG
    ratio = count * PATCH_IMG / patches
    rows_total = count * protos * groups
    place = lax.axis_index("dp").astype(jnp.int32).reshape(1)
    centre = centre.reshape(1, columns)

    def proto_swap(x, k):
        return lax.ppermute(x, "proto", xor_pairs(protos, k))

    def dp_swap(x, k):
        return lax.ppermute(x, "dp", xor_pairs(groups, k))

    pack, raw, inv = pick_rows(masked_rows, patch_image, student_patch[0], teacher_patch[0])
    near = [proto_swap(pack, k) for k in range(2, protos, 2)]
    ws, wt = round_protos(student_proto, teacher_proto)
    near, ws, wt = lax.optimization_barrier((near, ws, wt))
    own = jnp.concatenate([pack] + near, axis=0)
    other = proto_swap(own, 1)
    far = [dp_swap(own, k) for k in range(1, groups)]

    stats = first_pass(own, other, ws, wt, centre, student_proto, teacher_proto, count)
    stats = pl.pallas_call(
        core_join_kernel,
        out_shape=jax.ShapeDtypeStruct(stats.shape, f32),
        compiler_params=params(3),
        cost_estimate=cost(0, 1 << 20),
        name="core_join",
    )(stats, proto_swap(stats, 1))
    stats, *far = lax.optimization_barrier((stats, *far))
    far_other = [proto_swap(x, 1) for x in far]
    packs = [own, other]
    for pair in zip(far, far_other):
        packs += list(pair)
    us, ut, flipped, own_ws, own_wt = lay_rows(place, packs, student_proto, teacher_proto, count)

    own_centre = lax.dynamic_slice_in_dim(centre, place[0] * share, share, 1)
    near = [proto_swap(stats, k) for k in range(2, protos, 2)]
    stats, loss_own = pl.pallas_call(
        functools.partial(final_join_kernel, count=count, images=images, ratio=ratio),
        out_shape=[jax.ShapeDtypeStruct(stats.shape, f32), jax.ShapeDtypeStruct((8, 128), f32)],
        compiler_params=params(3),
        cost_estimate=cost(0, 1 << 20),
        name="final_join",
    )(stats, *near, own, other)
    all_stats = [stats] + [dp_swap(stats, k) for k in range(1, groups)]

    carry = [loss_own]
    sent = []
    for index in range(CHUNKS):
        out = second_pass(
            place, us, ut, flipped, own_ws, own_wt, own_centre, all_stats, carry, student_proto, teacher_proto, index, CHUNKS, count
        )
        if not index:
            (slab_s, slab_t), out = out[-2:], out[:-2]
        grads, carry = out[:groups], out[: groups - 1 : -1]
        if index + 1 < CHUNKS:
            sent.append([grads[0]] + [dp_swap(grads[k], k) for k in range(1, groups)])
    loss, send, keep = carry
    send, sent = lax.optimization_barrier((send, sent))
    depth = protos // 2
    out = core_sum(keep, proto_swap(send, 1), loss, depth)
    got = [proto_swap(out[k], 2 * k) for k in range(1, depth)]
    sent.append([grads[0]] + [dp_swap(grads[k], k) for k in range(1, groups)])
    jobs = {(k, index): grad for index, chunk in enumerate(sent) for k, grad in enumerate(chunk)}
    late = {job: jobs.pop(job) for job in list(jobs) if job[0] and job[1] == CHUNKS - 1}
    done = optimizer(place, jobs, slab_s, slab_t, first_moment, second_moment, None, share)
    got, done = lax.optimization_barrier((got, done))
    out = axis_sum(out[0], out[-1], got, groups)
    got = [dp_swap(out[k], k) for k in range(1, groups)]
    done = optimizer(place, late, slab_s, slab_t, first_moment, second_moment, done, share)
    got, done = lax.optimization_barrier((got, done))
    row_grad, total = pl.pallas_call(
        functools.partial(row_kernel, sources=len(got), rows_total=rows_total),
        out_shape=[jax.ShapeDtypeStruct((count, width), f32), jax.ShapeDtypeStruct((1, 1), f32)],
        out_specs=[pl.BlockSpec(memory_space=pltpu.VMEM), pl.BlockSpec(memory_space=pltpu.SMEM)],
        compiler_params=params(3),
        cost_estimate=cost(0, 1 << 20),
        name="row_grad",
    )(out[0], out[-1], raw, inv, *got)
    new_student, new_first, new_second, new_teacher = done
    return (row_grad[None], new_student, new_first, new_second, new_teacher, total.reshape(()))


def solution(mesh):
    in_specs = (
        P("dp", "proto", None),
        P("dp", "proto", None),
        P("dp", "proto"),
        P("dp", "proto"),
        P(None, "proto"),
        P(None, "proto"),
        P("dp", "proto"),
        P("dp", "proto"),
        P("proto"),
    )
    out_specs = (
        P("dp", "proto", None),
        P("dp", "proto"),
        P("dp", "proto"),
        P("dp", "proto"),
        P("dp", "proto"),
        P(),
    )
    return jax.shard_map(local, mesh=mesh, in_specs=in_specs, out_specs=out_specs, check_vma=False)
```

```python
import functools

import jax
import jax.numpy as jnp
from jax import lax
from jax.experimental import pallas as pl
from jax.experimental.pallas import tpu as pltpu
from jax.sharding import PartitionSpec as P

PATCH_IMG = 256

student_temp = 0.1
teacher_temp = 0.07
beta_one = 0.9
beta_two = 0.999
fix_one = 0.9999734386011124
fix_two = 0.09520785288629038
learn_rate = 0.002
decay_rate = 0.04
teacher_keep = 0.994

log2_e = 1.4426950408889634
ln_2 = 0.6931471805599453
least = 2.0**-60
most = 2.0**120
scale_s = log2_e / student_temp
scale_t = log2_e / teacher_temp

f32 = jnp.float32
bf16 = jnp.bfloat16
PAD = 16
CHUNKS = 2


def params(mebibytes):
    return pltpu.CompilerParams(vmem_limit_bytes=mebibytes << 20)


def cost(flops, moved):
    return pl.CostEstimate(flops=flops, bytes_accessed=moved, transcendentals=0)


def in_hbm(x):
    return pltpu.with_memory_space_constraint(x, pltpu.HBM)


def xor_pairs(size, k):
    return [(i, i ^ k) for i in range(size)]


def pick_kernel(rows_ref, image_ref, student_ref, teacher_ref, pack_ref, raw_ref, inv_ref):
    patches, width = student_ref.shape
    count = rows_ref.shape[1]
    hot = lax.broadcasted_iota(jnp.int32, (patches, count), 0) == rows_ref[...]
    hot = jnp.where(hot, 1.0, 0.0).astype(bf16)

    def pick(table):
        return lax.dot_general(hot, table, (((0,), (0,)), ((), ())), preferred_element_type=f32)

    def unit(raw):
        inverse = lax.rsqrt(jnp.sum(raw * raw, axis=-1, keepdims=True) + 1e-06)
        return raw * inverse, inverse

    raw_s = pick(student_ref[...])
    unit_s, inv_s = unit(raw_s)
    unit_t, _ = unit(pick(teacher_ref[...]))
    raw_ref[...] = raw_s
    inv_ref[...] = jnp.broadcast_to(inv_s, inv_ref.shape)
    pack_ref[0:count, :] = unit_s.astype(bf16)
    pack_ref[count : 2 * count, :] = unit_t.astype(bf16)
    images = jnp.broadcast_to(image_ref[...].astype(f32), (PAD, patches)).astype(bf16)
    ids = jnp.dot(images, hot, preferred_element_type=f32)
    pack_ref[2 * count :, :] = jnp.zeros((PAD, width), bf16)
    pack_ref[2 * count :, 0:count] = ids.astype(bf16)


def pick_rows(rows, image, student, teacher):
    patches, width = student.shape
    count = rows.shape[1]
    return pl.pallas_call(
        pick_kernel,
        out_shape=[
            jax.ShapeDtypeStruct((2 * count + PAD, width), bf16),
            jax.ShapeDtypeStruct((count, width), f32),
            jax.ShapeDtypeStruct((count, 128), f32),
        ],
        compiler_params=params(2),
        cost_estimate=cost(0, 1 << 20),
        name="pick_rows",
    )(*map(in_hbm, (rows, image, student, teacher)))


def round_kernel(s_hbm, t_hbm, ws, wt, buffer, sem, *, tile, depth):
    steps = ws.shape[1] // tile

    def copies(j):
        k = j % depth
        span = pl.ds(j * tile, tile)
        return [pltpu.make_async_copy(hbm.at[:, span], buffer.at[i, k], sem.at[i, k]) for i, hbm in enumerate((s_hbm, t_hbm))]

    for j in range(min(depth - 1, steps)):
        for copy in copies(j):
            copy.start()
    for j in range(steps):
        if j + depth - 1 < steps:
            for copy in copies(j + depth - 1):
                copy.start()
        for i, (copy, out) in enumerate(zip(copies(j), (ws, wt))):
            copy.wait()
            out[:, j * tile : (j + 1) * tile] = buffer[i, j % depth].astype(bf16)


def round_protos(student, teacher):
    width, cols = student.shape
    half = cols // 2
    tile = min(half, 1024)
    depth = 4
    return pl.pallas_call(
        functools.partial(round_kernel, tile=tile, depth=depth),
        in_specs=[pl.BlockSpec(memory_space=pltpu.HBM)] * 2,
        out_specs=[pl.BlockSpec(memory_space=pltpu.VMEM)] * 2,
        out_shape=[jax.ShapeDtypeStruct((width, half), bf16)] * 2,
        scratch_shapes=[pltpu.VMEM((2, depth, width, tile), f32), pltpu.SemaphoreType.DMA((2, depth))],
        compiler_params=params(10),
        cost_estimate=cost(0, 12 * width * half),
        name="round_protos",
    )(in_hbm(student), in_hbm(teacher))


def first_kernel(
    own_ref, other_ref, ws_ref, wt_ref, centre_ref, s_hbm, t_hbm, out_ref, us, ut, ms, ss, mt, st, rest, sem, *, count
):
    pack = 2 * count + PAD
    rows = us.shape[0]
    half = rows // 2
    cols = ws_ref.shape[1]
    tile = min(cols, 1024)
    unroll = 2 if cols % (2 * tile) == 0 else 1
    copies = []
    for j in range(cols // tile):
        for i, hbm in enumerate((s_hbm, t_hbm)):
            span = slice(j * tile, (j + 1) * tile)
            copies.append(pltpu.make_async_copy(hbm.at[:, pl.ds(cols + j * tile, tile)], rest.at[i, :, span], sem.at[i, j]))
            copies[-1].start()
    for c, ref in enumerate((own_ref, other_ref)):
        for z in range(half // count):
            at = c * half + z * count
            us[at : at + count, :] = ref[z * pack : z * pack + count, :]
            ut[at : at + count, :] = ref[z * pack + count : z * pack + 2 * count, :]

    block = min(rows, 512)

    def sweep(update, second):
        @pl.loop(0, cols // (tile * unroll))
        def _(j):
            for u in range(unroll):
                span = pl.ds(pl.multiple_of((j * unroll + u) * tile, tile), tile)
                if second:
                    ws = rest[0, :, span].astype(bf16)
                    wt = rest[1, :, span].astype(bf16)
                    place = pl.ds(pl.multiple_of(cols + (j * unroll + u) * tile, tile), tile)
                else:
                    ws = ws_ref[:, span]
                    wt = wt_ref[:, span]
                    place = span
                shift = centre_ref[:, place] * scale_t
                for r in range(rows // block):
                    at = slice(r * block, (r + 1) * block)
                    zs = jnp.dot(us[at, :], ws, preferred_element_type=f32)
                    update([zs[:, i : i + 128] * scale_s for i in range(0, tile, 128)], ms, ss, at)
                    zt = jnp.dot(ut[at, :], wt, preferred_element_type=f32)
                    update([zt[:, i : i + 128] * scale_t - shift[:, i : i + 128] for i in range(0, tile, 128)], mt, st, at)

    def plain(parts, m_ref, s_ref, at):
        s_ref[at, :] += functools.reduce(jnp.add, [jnp.exp2(part) for part in parts])

    def running(parts, m_ref, s_ref, at):
        old = m_ref[at, :]
        new = functools.reduce(jnp.maximum, parts, old)
        total = functools.reduce(jnp.add, [jnp.exp2(part - new) for part in parts])
        s_ref[at, :] = s_ref[at, :] * jnp.exp2(old - new) + total
        m_ref[at, :] = new

    for m, s in ((ms, ss), (mt, st)):
        m[...] = jnp.zeros_like(m)
        s[...] = jnp.zeros_like(s)
    sweep(plain, False)
    for copy in copies:
        copy.wait()
    sweep(plain, True)
    far = jnp.zeros((rows, 1), f32)
    for s in (ss, st):
        total = jnp.sum(s[...], axis=1, keepdims=True)
        far = jnp.maximum(far, jnp.where((total > least) & (total < most), 0.0, 1.0))

    @pl.when(jnp.max(far) > 0.5)
    def _():
        for m, s in ((ms, ss), (mt, st)):
            m[...] = jnp.full_like(m, -jnp.inf)
            s[...] = jnp.zeros_like(s)
        sweep(running, False)
        sweep(running, True)

    out_ref[...] = jnp.zeros_like(out_ref)
    for k, (m, s) in enumerate(((ms, ss), (mt, st))):
        lanes = m[...]
        peak = jnp.max(lanes, axis=1, keepdims=True)
        total = jnp.sum(s[...] * jnp.exp2(lanes - peak), axis=1, keepdims=True)
        lse = jnp.broadcast_to(peak + jnp.log2(total), lanes.shape)
        out_ref[k : k + 1, :] = jnp.transpose(lse)[0:1, :]


def first_pass(own, other, ws, wt, centre, student, teacher, count):
    width, cols = ws.shape
    tile = min(cols, 1024)
    rows = 2 * own.shape[0] // (2 * count + PAD) * count
    return pl.pallas_call(
        functools.partial(first_kernel, count=count),
        in_specs=[pl.BlockSpec(memory_space=pltpu.VMEM)] * 5 + [pl.BlockSpec(memory_space=pltpu.HBM)] * 2,
        out_shape=jax.ShapeDtypeStruct((8, rows), f32),
        scratch_shapes=[pltpu.VMEM((rows, width), bf16)] * 2
        + [pltpu.VMEM((rows, 128), f32)] * 4
        + [pltpu.VMEM((2, width, cols), f32), pltpu.SemaphoreType.DMA((2, cols // tile))],
        compiler_params=params((rows * (2 * width + 2048) + 8 * width * cols >> 20) + 7),
        cost_estimate=cost(8 * rows * width * cols, 12 * width * cols),
        name="first_pass",
    )(own, other, ws, wt, centre, in_hbm(student), in_hbm(teacher))


def join(parts):
    peak = functools.reduce(jnp.maximum, parts)
    total = functools.reduce(jnp.add, [jnp.exp2(part - peak) for part in parts])
    return peak + jnp.log2(total)


def swap_blocks(x, k, size):
    n = x.shape[1] // size
    return jnp.concatenate([x[:, (j ^ k) * size : ((j ^ k) + 1) * size] for j in range(n)], axis=1)


def core_join_kernel(own_ref, other_ref, out_ref):
    half = own_ref.shape[1] // 2
    out_ref[...] = join([own_ref[...], swap_blocks(other_ref[...], 1, half)])


def final_join_kernel(*refs, count, images, ratio):
    stats, (own_ref, other_ref, _), (out_ref, loss_ref) = refs[:-5], refs[-5:-2], refs[-2:]
    rows = stats[0].shape[1]
    pack = 2 * count + PAD
    lse = join([swap_blocks(ref[...], k, count) for k, ref in enumerate(stats)])
    ids = jnp.concatenate(
        [
            ref[z * pack + 2 * count : (z + 1) * pack, 0:count].astype(f32)[0:8, :]
            for ref in (own_ref, other_ref)
            for z in range(rows // (2 * count))
        ],
        axis=1,
    )
    per_row = jnp.zeros_like(ids)
    for label in range(images):
        match = jnp.where(ids == label, 1.0, 0.0)
        per_row += match * jnp.sum(match, axis=1, keepdims=True)
    weight = ratio / per_row
    out_ref[...] = lse - jnp.log2(weight / student_temp)
    own = jnp.sum(weight[0:1, 0:count] * lse[0:1, 0:count] * ln_2, axis=1, keepdims=True)
    loss_ref[...] = jnp.broadcast_to(own, loss_ref.shape)


def share_kernel(place_ref, _, s_hbm, t_hbm, out_s, out_t, done_ref, buffer, rounded, sem, *, tile):
    share = out_s.shape[1]
    pairs = ((s_hbm, out_s), (t_hbm, out_t))
    jobs = [(i, j) for j in range(share // tile) for i in range(2)]
    leaving = []

    def fetch(i, j):
        span = pl.ds(pl.multiple_of(place_ref[0] * share + j * tile, tile), tile)
        return pltpu.make_async_copy(pairs[i][0].at[:, span], buffer.at[i, j], sem.at[0, i, j])

    for job in jobs:
        fetch(*job).start()
    for i, j in jobs:
        fetch(i, j).wait()
        rounded[i, j] = buffer[i, j].astype(bf16)
        leaving.append(
            pltpu.make_async_copy(rounded.at[i, j], pairs[i][1].at[:, pl.ds(j * tile, tile)], sem.at[1, i, j])
        )
        leaving[-1].start()
    done_ref[...] = jnp.zeros_like(done_ref)
    for copy in leaving:
        copy.wait()


def round_share(place, stats, student, teacher, groups):
    width, cols = student.shape
    share = cols // groups
    tile = min(share, 1024)
    steps = share // tile
    vmem = pl.BlockSpec(memory_space=pltpu.VMEM)
    hbm = pl.BlockSpec(memory_space=pltpu.HBM)
    return pl.pallas_call(
        functools.partial(share_kernel, tile=tile),
        in_specs=[pl.BlockSpec(memory_space=pltpu.SMEM), vmem, hbm, hbm],
        out_specs=[hbm, hbm, vmem],
        out_shape=[pltpu.HBM((width, share), bf16)] * 2 + [jax.ShapeDtypeStruct((8, 128), f32)],
        scratch_shapes=[
            pltpu.VMEM((2, steps, width, tile), f32),
            pltpu.VMEM((2, steps, width, tile), bf16),
            pltpu.SemaphoreType.DMA((2, 2, steps)),
        ],
        compiler_params=params((12 * width * share >> 20) + 2),
        cost_estimate=cost(0, 12 * width * share),
        name="round_share",
    )(place, stats, in_hbm(student), in_hbm(teacher))


def lay_kernel(place_ref, *refs, count, groups):
    packs, (s_hbm, t_hbm), refs = refs[: 2 * groups], refs[2 * groups : 2 * groups + 2], refs[2 * groups + 2 :]
    us, ut, flipped, own_s, own_t, turned, sem = refs
    share = own_s.shape[1]
    tile = share // sem.shape[1]
    copies = []
    for j in range(share // tile):
        inner = pl.ds(j * tile, tile)
        for i, (hbm, own) in enumerate(((s_hbm, own_s), (t_hbm, own_t))):
            copies.append(pltpu.make_async_copy(hbm.at[:, inner], own.at[:, inner], sem.at[i, j]))
            copies[-1].start()
    pack = 2 * count + PAD
    at = 0
    for ref in packs:
        for z in range(ref.shape[0] // pack):
            us[at : at + count, :] = ref[z * pack : z * pack + count, :]
            ut[at : at + count, :] = ref[z * pack + count : z * pack + 2 * count, :]
            at += count
    width = us.shape[1]
    turned[...] = jnp.transpose(us[...])
    slab = width // groups
    for k in range(groups):
        start = pl.multiple_of((place_ref[0] ^ k) * slab, slab)
        flipped[k * slab : (k + 1) * slab, :] = turned[pl.ds(start, slab), :]
    for copy in copies:
        copy.wait()


def lay_rows(place, packs, own_s, own_t, count):
    groups = len(packs) // 2
    width, share = own_s.shape
    tile = min(share, 1024)
    rows = 2 * groups * (packs[0].shape[0] // (2 * count + PAD)) * count
    vmem = pl.BlockSpec(memory_space=pltpu.VMEM)
    hbm = pl.BlockSpec(memory_space=pltpu.HBM)
    return pl.pallas_call(
        functools.partial(lay_kernel, count=count, groups=groups),
        in_specs=[pl.BlockSpec(memory_space=pltpu.SMEM)] + [vmem] * len(packs) + [hbm] * 2,
        out_shape=[jax.ShapeDtypeStruct((rows, width), bf16)] * 2
        + [jax.ShapeDtypeStruct((width, rows), bf16)]
        + [jax.ShapeDtypeStruct((width, share), bf16)] * 2,
        out_specs=[vmem] * 5,
        scratch_shapes=[
            pltpu.VMEM((width, rows), bf16),
            pltpu.SemaphoreType.DMA((2, share // tile)),
        ],
        compiler_params=params((width * rows * 2 >> 20) + 2),
        cost_estimate=cost(0, 4 << 20),
        name="lay_rows",
    )(place, *packs, in_hbm(own_s), in_hbm(own_t))


def pieces(value):
    rows = lax.broadcasted_iota(jnp.int32, (PAD, 256), 0)
    out = jnp.zeros((PAD, 256), f32)
    for k in range(3):
        piece = value.astype(bf16).astype(f32)
        out = jnp.where(rows == k, piece, out)
        value = value - piece
    return out.astype(bf16)


def joined(block):
    return jnp.sum(block[:, 0:1].astype(f32), axis=0, keepdims=True)


def second_kernel(us, ut, flipped, ws_ref, wt_ref, centre_ref, *refs, groups, index, chunk, last, count):
    stats, refs = refs[:groups], refs[groups:]
    seed_ref, refs = refs[0], refs[1:]
    if index:
        carry_ref, refs = refs[0], refs[1:]
    else:
        (place_ref, *protos), refs = refs[:3], refs[3:]
        sem, refs = refs[-1], refs[:-1]
    grads, refs = refs[:groups], refs[groups:]
    if last:
        keep_ref, send_ref, loss_ref, total, loss_sum, shift_s, shift_t = refs
    else:
        total, loss_ref, *slabs, loss_sum, shift_s, shift_t = refs
    rows, width = us.shape
    group_rows = rows // groups
    slab = width // groups
    copies = []
    if not index:
        start = pl.multiple_of(place_ref[0] * slab, slab)
        for i, (hbm, out) in enumerate(zip(protos, slabs)):
            copies.append(pltpu.make_async_copy(hbm.at[pl.ds(start, slab), :], out, sem.at[i]))
            copies[-1].start()
    tile = min(chunk, 512)
    steps = chunk // tile

    total[...] = carry_ref[...] if index else jnp.zeros_like(total)
    loss_sum[...] = jnp.zeros_like(loss_sum)
    for g in range(groups):
        at = slice(g * group_rows, (g + 1) * group_rows)
        for k, shift in enumerate((shift_s, shift_t)):
            shift[at, :] = jnp.transpose(jnp.broadcast_to(stats[g][k : k + 1, :], (128, group_rows)))

    block = min(group_rows, 256)
    places = [slice(r * block, (r + 1) * block) for r in range(rows // block)]

    @pl.loop(0, steps)
    def _(j):
        span = pl.ds(pl.multiple_of(index * chunk + j * tile, tile), tile)
        ws = ws_ref[:, span]
        wt = wt_ref[:, span]
        centre = centre_ref[:, span] * scale_t

        def products(at):
            return (
                jnp.dot(us[at, :], ws, preferred_element_type=f32),
                jnp.dot(ut[at, :], wt, preferred_element_type=f32),
            )

        ready = products(places[0])
        grad = None
        for r, at in enumerate(places):
            zs, zt = ready
            if r + 1 < len(places):
                ready = products(places[r + 1])
            down_s, down_t = shift_s[at, :], shift_t[at, :]
            parts = []
            loss = None
            for i in range(0, tile, 128):
                zsi = zs[:, i : i + 128]
                ps = jnp.exp2(zsi * scale_s - down_s)
                pt = jnp.exp2(zt[:, i : i + 128] * scale_t - centre[:, i : i + 128] - down_t)
                cross = pt * zsi
                loss = cross if loss is None else loss + cross
                parts.append((ps - pt).astype(bf16))
            loss_sum[...] += jnp.sum(loss.reshape(block // 8, 8, 128), axis=0)
            logit = jnp.concatenate(parts, axis=1)
            total[at, :] += lax.dot_general(logit, ws, (((1,), (1,)), ((), ())), preferred_element_type=f32)
            part = jnp.dot(flipped[:, at], logit, preferred_element_type=f32)
            grad = part if grad is None else grad + part
        out = pl.ds(pl.multiple_of(j * tile, tile), tile)
        for k in range(groups):
            grads[k][:, out] = grad[k * slab : (k + 1) * slab, :].astype(bf16)

    done = jnp.sum(jnp.sum(loss_sum[...], axis=1, keepdims=True), axis=0, keepdims=True)
    loss = seed_ref[0:1, 0:1] - done
    loss_ref[...] = jnp.broadcast_to(loss, loss_ref.shape)
    for copy in copies:
        copy.wait()
    if last:
        send_ref[rows // 2 :, :] = pieces(loss)
        depth = group_rows // (2 * count)
        for g in range(groups):
            for c, ref in enumerate((keep_ref, send_ref)):
                for z in range(depth):
                    src = g * group_rows + (c * depth + z) * count
                    dst = (z * groups + g) * count
                    ref[dst : dst + count, :] = total[src : src + count, :].astype(ref.dtype)


def second_pass(place, us, ut, flipped, ws, wt, centre, stats, carry, student, teacher, index, chunks, count):
    rows, width = us.shape
    groups = len(stats)
    slab = width // groups
    chunk = centre.shape[1] // chunks
    last = index == chunks - 1
    args = [us, ut, flipped, ws, wt, centre, *stats, *carry]
    in_specs = [pl.BlockSpec(memory_space=pltpu.VMEM)] * len(args)
    out_shape = [jax.ShapeDtypeStruct((slab, chunk), bf16)] * groups
    scratch = [pltpu.VMEM((8, 128), f32)] + [pltpu.VMEM((rows, 128), f32)] * 2
    if last:
        out_shape += [jax.ShapeDtypeStruct((rows // 2, width), f32), jax.ShapeDtypeStruct((rows // 2 + PAD, width), bf16)]
        scratch = [pltpu.VMEM((rows, width), f32)] + scratch
    else:
        out_shape += [jax.ShapeDtypeStruct((rows, width), f32)]
    out_shape += [jax.ShapeDtypeStruct((8, 128), f32)]
    if not index:
        args += [place, in_hbm(student), in_hbm(teacher)]
        in_specs += [pl.BlockSpec(memory_space=pltpu.SMEM)] + [pl.BlockSpec(memory_space=pltpu.HBM)] * 2
        out_shape += [jax.ShapeDtypeStruct((slab, student.shape[1]), f32)] * 2
        scratch += [pltpu.SemaphoreType.DMA((2,))]
    held = 2 * rows * 128 * 4 + 2 * rows * width * 4
    return pl.pallas_call(
        functools.partial(second_kernel, groups=groups, index=index, chunk=chunk, last=last, count=count),
        in_specs=in_specs,
        out_specs=[pl.BlockSpec(memory_space=pltpu.VMEM)] * len(out_shape),
        out_shape=out_shape,
        scratch_shapes=scratch,
        compiler_params=params((held >> 20) + 4),
        cost_estimate=cost(8 * rows * width * chunk, 8 * width * chunk),
        name="second_pass",
    )(*args)


def core_sum_kernel(keep_ref, got_ref, loss_ref, *outs, blocks):
    size = keep_ref.shape[0] // blocks
    loss = loss_ref[0:1, 0:1] + joined(got_ref[keep_ref.shape[0] :, :])
    for k in range(blocks):
        at = slice(k * size, (k + 1) * size)
        outs[k][0:size, :] = (keep_ref[at, :] + got_ref[at, :].astype(f32)).astype(outs[k].dtype)
        if k:
            outs[k][size:, :] = pieces(loss)
    outs[-1][...] = jnp.broadcast_to(loss, outs[-1].shape)


def core_sum(keep, got, loss, blocks):
    rows, width = keep.shape
    size = rows // blocks
    return pl.pallas_call(
        functools.partial(core_sum_kernel, blocks=blocks),
        out_shape=[jax.ShapeDtypeStruct((size, width), f32)]
        + [jax.ShapeDtypeStruct((size + PAD, width), bf16)] * (blocks - 1)
        + [jax.ShapeDtypeStruct((8, 128), f32)],
        compiler_params=params(3),
        cost_estimate=cost(0, 1 << 20),
        name="core_sum",
    )(keep, got, loss)


def axis_sum_kernel(keep_ref, loss_ref, *refs, blocks, sources):
    got, outs = refs[:sources], refs[sources:]
    rows = keep_ref.shape[0]
    size = rows // blocks
    loss = loss_ref[0:1, 0:1]
    for ref in got:
        loss = loss + joined(ref[rows:, :])
    for k in range(blocks):
        at = slice(k * size, (k + 1) * size)
        total = keep_ref[at, :]
        for ref in got:
            total = total + ref[at, :].astype(f32)
        outs[k][0:size, :] = total.astype(outs[k].dtype)
        if k:
            outs[k][size:, :] = pieces(loss)
    outs[-1][...] = jnp.broadcast_to(loss, outs[-1].shape)


def axis_sum(keep, loss, got, blocks):
    rows, width = keep.shape
    size = rows // blocks
    return pl.pallas_call(
        functools.partial(axis_sum_kernel, blocks=blocks, sources=len(got)),
        out_shape=[jax.ShapeDtypeStruct((size, width), f32)]
        + [jax.ShapeDtypeStruct((size + PAD, width), bf16)] * (blocks - 1)
        + [jax.ShapeDtypeStruct((8, 128), f32)],
        compiler_params=params(3),
        cost_estimate=cost(0, 1 << 20),
        name="axis_sum",
    )(keep, loss, *got)


def row_kernel(keep_ref, loss_ref, raw_ref, inv_ref, *refs, sources, rows_total):
    got, (out_ref, total_ref) = refs[:sources], refs[sources:]
    rows = keep_ref.shape[0]
    loss = loss_ref[0:1, 0:1]
    grad = keep_ref[...]
    for ref in got:
        loss = loss + joined(ref[rows:, :])
        grad = grad + ref[0:rows, :].astype(f32)
    raw = raw_ref[...]
    inv = inv_ref[:, 0:1]
    out_ref[...] = inv * grad - inv * inv * inv * raw * jnp.sum(raw * grad, axis=-1, keepdims=True)
    total_ref[0, 0] = jnp.sum(loss) / rows_total


def step_kernel(place_ref, *refs, jobs, chunk, share):
    grads = refs[: len(jobs)]
    student_ref, teacher_ref, first_ref, second_ref = refs[len(jobs) : len(jobs) + 4]
    outs, stage, sem = refs[-6:-2], refs[-2], refs[-1]
    copies = []
    for k, (source, index) in enumerate(jobs):
        span = pl.ds(pl.multiple_of((place_ref[0] ^ source) * share + index * chunk, chunk), chunk)
        grad = grads[k][...].astype(f32)
        first = beta_one * first_ref[:, span] + (1.0 - beta_one) * grad
        second = beta_two * second_ref[:, span] + (1.0 - beta_two) * grad * grad
        step = first / fix_one / (jnp.sqrt(second / fix_two) + 1e-08)
        student = student_ref[:, span]
        student = student - learn_rate * (step + decay_rate * student)
        teacher = teacher_keep * teacher_ref[:, span] + (1.0 - teacher_keep) * student
        for i, value in enumerate((student, first, second, teacher)):
            stage[k, i] = value
            copies.append(pltpu.make_async_copy(stage.at[k, i], outs[i].at[:, span], sem.at[k, i]))
            copies[-1].start()
    for copy in copies:
        copy.wait()


def optimizer(place, jobs, student, teacher, first, second, done, share):
    jobs, grads = list(jobs), list(jobs.values())
    slab, total = first.shape
    chunk = grads[0].shape[1]
    vmem = pl.BlockSpec(memory_space=pltpu.VMEM)
    hbm = pl.BlockSpec(memory_space=pltpu.HBM)
    in_specs = [pl.BlockSpec(memory_space=pltpu.SMEM)] + [vmem] * (len(jobs) + 4)
    args = [place, *grads, student, teacher, first, second]
    aliases = {}
    if done is not None:
        aliases = {len(args) + i: i for i in range(4)}
        in_specs += [hbm] * 4
        args += list(done)
    return pl.pallas_call(
        functools.partial(step_kernel, jobs=jobs, chunk=chunk, share=share),
        in_specs=in_specs,
        out_specs=[hbm] * 4,
        out_shape=[jax.ShapeDtypeStruct((slab, total), f32)] * 4,
        scratch_shapes=[pltpu.VMEM((len(jobs), 4, slab, chunk), f32), pltpu.SemaphoreType.DMA((len(jobs), 4))],
        input_output_aliases=aliases,
        compiler_params=params((len(jobs) * 16 * slab * chunk >> 20) + 3),
        cost_estimate=cost(20 * slab * len(jobs) * chunk, 16 * slab * len(jobs) * chunk),
        name="optimizer",
    )(*args)


def local(
    student_patch,
    teacher_patch,
    patch_image,
    masked_rows,
    student_proto,
    teacher_proto,
    first_moment,
    second_moment,
    centre,
):
    count = masked_rows.shape[1]
    patches, width = student_patch.shape[1:]
    protos = lax.axis_size("proto")
    groups = lax.axis_size("dp")
    columns = student_proto.shape[1]
    share = columns // groups
    images = patches * protos // PATCH_IMG
    ratio = count * PATCH_IMG / patches
    rows_total = count * protos * groups
    place = lax.axis_index("dp").astype(jnp.int32).reshape(1)
    centre = centre.reshape(1, columns)

    def proto_swap(x, k):
        return lax.ppermute(x, "proto", xor_pairs(protos, k))

    def dp_swap(x, k):
        return lax.ppermute(x, "dp", xor_pairs(groups, k))

    pack, raw, inv = pick_rows(masked_rows, patch_image, student_patch[0], teacher_patch[0])
    near = [proto_swap(pack, k) for k in range(2, protos, 2)]
    ws, wt = round_protos(student_proto, teacher_proto)
    near, ws, wt = lax.optimization_barrier((near, ws, wt))
    own = jnp.concatenate([pack] + near, axis=0)
    other = proto_swap(own, 1)
    far = [dp_swap(own, k) for k in range(1, groups)]

    stats = first_pass(own, other, ws, wt, centre, student_proto, teacher_proto, count)
    stats = pl.pallas_call(
        core_join_kernel,
        out_shape=jax.ShapeDtypeStruct(stats.shape, f32),
        compiler_params=params(3),
        cost_estimate=cost(0, 1 << 20),
        name="core_join",
    )(stats, proto_swap(stats, 1))
    stats, *far = lax.optimization_barrier((stats, *far))
    far_other = [proto_swap(x, 1) for x in far]
    packs = [own, other]
    for pair in zip(far, far_other):
        packs += list(pair)
    share_s, share_t, rounded = round_share(place, stats, student_proto, teacher_proto, groups)
    us, ut, flipped, own_ws, own_wt = lay_rows(place, packs, share_s, share_t, count)

    own_centre = lax.dynamic_slice_in_dim(centre, place[0] * share, share, 1)
    near = [proto_swap(stats, k) for k in range(2, protos, 2)]
    stats, loss_own = pl.pallas_call(
        functools.partial(final_join_kernel, count=count, images=images, ratio=ratio),
        out_shape=[jax.ShapeDtypeStruct(stats.shape, f32), jax.ShapeDtypeStruct((8, 128), f32)],
        compiler_params=params(3),
        cost_estimate=cost(0, 1 << 20),
        name="final_join",
    )(stats, *near, own, other, rounded)
    all_stats = [stats] + [dp_swap(stats, k) for k in range(1, groups)]

    carry = [loss_own]
    sent = []
    for index in range(CHUNKS):
        out = second_pass(
            place, us, ut, flipped, own_ws, own_wt, own_centre, all_stats, carry, student_proto, teacher_proto, index, CHUNKS, count
        )
        if not index:
            (slab_s, slab_t), out = out[-2:], out[:-2]
        grads, carry = out[:groups], out[: groups - 1 : -1]
        if index + 1 < CHUNKS:
            sent.append([grads[0]] + [dp_swap(grads[k], k) for k in range(1, groups)])
    loss, send, keep = carry
    send, sent = lax.optimization_barrier((send, sent))
    depth = protos // 2
    out = core_sum(keep, proto_swap(send, 1), loss, depth)
    got = [proto_swap(out[k], 2 * k) for k in range(1, depth)]
    sent.append([grads[0]] + [dp_swap(grads[k], k) for k in range(1, groups)])
    jobs = {(k, index): grad for index, chunk in enumerate(sent) for k, grad in enumerate(chunk)}
    late = {job: jobs.pop(job) for job in list(jobs) if job[0] and job[1] == CHUNKS - 1}
    done = optimizer(place, jobs, slab_s, slab_t, first_moment, second_moment, None, share)
    got, done = lax.optimization_barrier((got, done))
    out = axis_sum(out[0], out[-1], got, groups)
    got = [dp_swap(out[k], k) for k in range(1, groups)]
    done = optimizer(place, late, slab_s, slab_t, first_moment, second_moment, done, share)
    got, done = lax.optimization_barrier((got, done))
    row_grad, total = pl.pallas_call(
        functools.partial(row_kernel, sources=len(got), rows_total=rows_total),
        out_shape=[jax.ShapeDtypeStruct((count, width), f32), jax.ShapeDtypeStruct((1, 1), f32)],
        out_specs=[pl.BlockSpec(memory_space=pltpu.VMEM), pl.BlockSpec(memory_space=pltpu.SMEM)],
        compiler_params=params(3),
        cost_estimate=cost(0, 1 << 20),
        name="row_grad",
    )(out[0], out[-1], raw, inv, *got)
    new_student, new_first, new_second, new_teacher = done
    return (row_grad[None], new_student, new_first, new_second, new_teacher, total.reshape(()))


def solution(mesh):
    in_specs = (
        P("dp", "proto", None),
        P("dp", "proto", None),
        P("dp", "proto"),
        P("dp", "proto"),
        P(None, "proto"),
        P(None, "proto"),
        P("dp", "proto"),
        P("dp", "proto"),
        P("proto"),
    )
    out_specs = (
        P("dp", "proto", None),
        P("dp", "proto"),
        P("dp", "proto"),
        P("dp", "proto"),
        P("dp", "proto"),
        P(),
    )
    return jax.shard_map(local, mesh=mesh, in_specs=in_specs, out_specs=out_specs, check_vma=False)
```
